128 devices in a mesh: tile: 8 (over y, core), seq: 16 (over z, x).
Axes of the slice: x: 4, y: 4, z: 4, core: 2. Of those that a mesh axis runs over, the one named last changes fastest.
Arguments:
- tokens: bfloat16 [128, 8, 16, 4, 1024], P(('tile', 'seq')), as said below
- levels: int32 [128, 8, 16, 4], P(('tile', 'seq')), may hold values from 0 to 5
- counts: int32 [8, 16, 128], replicated, may hold values from 1 to 4, 256 in all within a row
- level_table: bfloat16 [6, 1024], replicated, may hold values from -6 to 6
- norm_gain: float32 [1024], replicated, may hold values from 0.5 to 2
- project_weight: bfloat16 [16, 3, 64, 1024], replicated, may hold values from -0.1875 to 0.1875
- output_weight: bfloat16 [16, 64, 1024], replicated, may hold values from -0.1875 to 0.1875
- cotangent: bfloat16 [8, 4096, 1024], P('tile', 'seq'), may hold values from -6 to 6
Outputs:
- output: bfloat16 [8, 4096, 1024], P('tile', 'seq')
- token_grad: bfloat16 [128, 8, 16, 4, 1024], P(('tile', 'seq'))
- project_grad: float32 [16, 3, 64, 1024], P('seq', None, None, 'tile')
- output_grad: float32 [16, 64, 1024], P('seq', None, 'tile')
- gain_grad: float32 [1024], replicated
- table_grad: float32 [6, 1024], replicated
The draws below stay inside these ranges and needn't reach their ends.
Inputs may be any that keep to these rules, and one draw needn't show every extreme that they name: For each map and shard, the 128 tile counts sum to 256, and one of them is 4. `tokens`: features in slots at or past a tile's count are never read.
All inputs are finite; a program needn't handle non-finite values.
Results may differ from the reference program's by a relative error of at most 0.025.
Values may be sent and summed in bfloat16 or wider, within the bound.
No kernel may reach another device: no remote copies, remote signals or barrier semaphores. Data moves between devices by JAX's collectives and lax.ppermute only.
A program may use at most 128 MiB of HBM per device.

```python
import math
import jax
import jax.numpy as jnp
import numpy as np
from jax import lax

D = 1024
HEADS = 16
HD = 64
TOK_DEV = 256
LEVELS = 6
MAPS = 8
OWNERS = 128
SLOT = 4
SEQ_LEN = 4096
N_SEQ = 16


def draw_tokens(key, part):
    key = jax.random.fold_in(key, 7)
    first, second, third = jax.random.split(key, 3)
    shape = (OWNERS, MAPS, N_SEQ, SLOT, D)
    row_scale = jnp.exp(jax.random.uniform(second, (OWNERS, MAPS, N_SEQ, SLOT, 1), jnp.float32, -1.15, 1.15))
    column_scale = jnp.exp(jax.random.uniform(third, (D,), jnp.float32, -1.15, 1.15))
    base = jax.random.normal(first, shape, jnp.float32)
    return (base * row_scale * column_scale).astype(jnp.bfloat16)


def touch_ends(drawn, key, smallest, top_value):
    dims = drawn.shape
    index_at = [jax.random.randint(jax.random.fold_in(key, axis), (), 0, dims[axis]) for axis in range(len(dims))]
    drawn = drawn.at[tuple(index_at)].set(smallest)
    longest = dims.index(max(dims))
    index_at[longest] = (index_at[longest] + 1) % dims[longest]
    return drawn.at[tuple(index_at)].set(top_value)


def level_of(rng, extent, cuts, low, high):
    def one(axis_at, blocks):
        heights = jax.random.uniform(jax.random.fold_in(jax.random.fold_in(rng, 6), axis_at), (blocks,), jnp.float32, low / len(cuts), high / len(cuts))
        return jnp.repeat(jnp.exp(heights), extent[axis_at] // blocks).reshape((-1,) + (1,) * (len(extent) - axis_at - 1))

    gain = one(*cuts[0])
    for cut in cuts[1:]:
        gain = gain * one(*cut)
    return gain


def profile(count, total, most, lean):
    portions = [(1 << 20) // math.isqrt(standing ** lean) + 1 for standing in range(2, count + 1)]
    spare, given = total - most - (count - 1), [1] * (count - 1)
    while spare > 0:
        movable = [i for i in range(count - 1) if given[i] < most]
        mass, left = sum([portions[i] for i in movable]), spare
        for i in movable:
            extra = min(most - given[i], max(1, left * portions[i] // mass), spare)
            given[i] = given[i] + extra
            spare = spare - extra
    return np.array([most] + given)


def ragged(rng, amount, total, limit, slope):
    if amount == 2:
        one = jax.random.randint(rng, (), max(1, total - limit), min(limit, total - 1) + 1)
        return jnp.stack([one, total - one])
    tallies = jnp.asarray(profile(amount, total, limit, slope), jnp.int32)
    twos = (amount - 1) // 2
    source_of, sink = tallies[1:1 + 2 * twos:2], tallies[2:2 + 2 * twos:2]
    slack = jnp.minimum(source_of - 1, limit - sink)
    moved = jax.random.randint(jax.random.fold_in(rng, 1), (twos,), 0, 1 << 20) % (slack + 1)
    tallies = tallies.at[1:1 + 2 * twos:2].set(source_of - moved).at[2:2 + 2 * twos:2].set(sink + moved)
    return tallies[jax.random.permutation(jax.random.fold_in(rng, 2), amount)]


def scatter_about(own_key, shape, spread, bound, cuts=(), kind=jnp.bfloat16):
    loudness = level_of(own_key, shape, cuts, -0.22, 0.18) if cuts else 1.0
    values = jax.random.normal(own_key, shape, jnp.float32) * spread * loudness
    return jnp.minimum(jnp.maximum(values, -bound), bound).astype(kind)


def setup_inputs(seed: int = 0) -> dict:
    key_list = jax.random.split(jax.random.key(seed), 9)
    tokens = draw_tokens(jax.random.fold_in(key_list[8], 71), 0)
    levels = touch_ends(jax.random.randint(key_list[1], (OWNERS, MAPS, N_SEQ, SLOT), 0, LEVELS), jax.random.fold_in(key_list[1], 1), 0, LEVELS - 1).astype(jnp.int32)
    counts = jax.vmap(lambda own: ragged(own, OWNERS, TOK_DEV, SLOT, 2))(jax.random.split(key_list[2], MAPS * N_SEQ)).reshape((MAPS, N_SEQ, OWNERS)).astype(jnp.int32)
    level_table = scatter_about(key_list[3], (LEVELS, D), 1.0, 6.0)
    norm_gain = jnp.clip(jnp.exp(jax.random.uniform(key_list[4], (D,), jnp.float32, math.log(0.5), math.log(2.0))), 0.5, 2.0)
    project_weight = scatter_about(key_list[5], (HEADS, 3, HD, D), D ** -0.5, 0.1875)
    output_weight = scatter_about(key_list[6], (HEADS, HD, D), D ** -0.5, 0.1875)
    cotangent = scatter_about(key_list[7], (MAPS, SEQ_LEN, D), 1.0, 6.0, ((0, 8), (1, 16)))
    return dict(tokens=tokens, levels=levels, counts=counts, level_table=level_table, norm_gain=norm_gain, project_weight=project_weight, output_weight=output_weight, cotangent=cotangent)


EPSILON = 1e-05

def rounded(array):
    return lax.optimization_barrier(array.astype(jnp.bfloat16)).astype(jnp.float32)

def level_rows(levels, table):
    onehot = (levels[..., None] == jnp.arange(table.shape[0], dtype=jnp.int32)).astype(jnp.float32)
    return jnp.einsum('omsjl,ld->omsjd', onehot, table.astype(jnp.float32))

def pack_positions(counts, rows, slots):
    starts = (jnp.cumsum(counts) - counts).astype(jnp.int32)
    place = jnp.arange(rows, dtype=jnp.int32)
    before = (starts[None, :] <= place[:, None]).astype(jnp.int32)
    owner = (lax.optimization_barrier(jnp.sum(before, axis=1)) - 1).astype(jnp.int32)
    first = lax.optimization_barrier(jnp.max(jnp.where(before > 0, starts[None, :], 0), axis=1)).astype(jnp.int32)
    return (owner * slots + place - first).astype(jnp.int32)

def unpack_positions(counts, slots):
    starts = (jnp.cumsum(counts) - counts).astype(jnp.int32)
    within = jnp.arange(slots, dtype=jnp.int32)
    usable = within[None, :] < counts[:, None]
    return (jnp.where(usable, starts[:, None] + within[None, :], 0).astype(jnp.int32), usable)

def to_blocks(array, block):
    width, length = array.shape
    return array.reshape(width, length // block, block).transpose(1, 0, 2)

def from_blocks(array):
    count, width, block = array.shape
    return array.transpose(1, 0, 2).reshape(width, count * block)

def head_forward(query, keys, values, scale, shift):
    block = math.gcd(query.shape[1], 512)
    keys32 = keys.astype(jnp.float32)
    values32 = values.astype(jnp.float32)

    def one_block(rows):
        scores = jnp.einsum('ei,ej->ij', rows.astype(jnp.float32), keys32) * scale - shift
        weights = rounded(jax.nn.sigmoid(scores))
        return jnp.einsum('ij,ej->ei', weights, values32).astype(jnp.bfloat16)
    return from_blocks(lax.map(one_block, to_blocks(query, block)))

def head_backward(query, keys, values, grad_out, scale, shift):
    width, length = query.shape
    block = math.gcd(length, 512)
    keys32 = keys.astype(jnp.float32)
    values32 = values.astype(jnp.float32)

    def one_block(carry, pair):
        key_total, value_total = carry
        rows32 = pair[0].astype(jnp.float32)
        grads32 = pair[1].astype(jnp.float32)
        scores = jnp.einsum('ei,ej->ij', rows32, keys32) * scale - shift
        probs = jax.nn.sigmoid(scores)
        weights = rounded(probs)
        grad_weights = jnp.einsum('ei,ej->ij', grads32, values32)
        grad_scores = rounded(grad_weights * probs * (1.0 - probs))
        grad_query = (jnp.einsum('ij,ej->ei', grad_scores, keys32) * scale).astype(jnp.bfloat16)
        key_total = key_total + jnp.einsum('ij,ei->ej', grad_scores, rows32)
        value_total = value_total + jnp.einsum('ij,ei->ej', weights, grads32)
        return ((key_total, value_total), grad_query)
    zeros = jnp.zeros((width, length), jnp.float32)
    totals, grad_query = lax.scan(one_block, (zeros, zeros), (to_blocks(query, block), to_blocks(grad_out, block)))
    return (from_blocks(grad_query), (totals[0] * scale).astype(jnp.bfloat16), totals[1].astype(jnp.bfloat16))

def reference(tokens, levels, counts, level_table, norm_gain, project_weight, output_weight, cotangent):
    owners, maps, shards, slots, width = tokens.shape
    head_width = project_weight.shape[2]
    length = shards * TOK_DEV
    scale = 1.0 / math.sqrt(head_width)
    shift = math.log(length)
    factor = 1.0 / math.sqrt(maps * length)
    embedded = (tokens.astype(jnp.float32) + level_rows(levels, level_table)).astype(jnp.bfloat16)
    by_map = embedded.transpose(1, 2, 0, 3, 4).reshape(maps, shards, owners * slots, width)
    gain32 = norm_gain.astype(jnp.float32)
    project32 = project_weight.astype(jnp.float32)
    output32 = output_weight.astype(jnp.float32)

    def attend(triple):
        return head_forward(triple[0], triple[1], triple[2], scale, shift)

    def backward(quad):
        return jnp.stack(head_backward(quad[0], quad[1], quad[2], quad[3], scale, shift), axis=0)
    outputs = []
    owner_grads = []
    project_total = jnp.zeros(project_weight.shape, jnp.float32)
    output_total = jnp.zeros(output_weight.shape, jnp.float32)
    gain_total = jnp.zeros((width,), jnp.float32)
    for index in range(maps):
        pieces = []
        for shard in range(shards):
            positions = pack_positions(counts[index, shard], TOK_DEV, slots)
            pieces.append(jnp.take(by_map[index, shard], positions, axis=0))
        features = jnp.concatenate(pieces, axis=0)
        activations = features.astype(jnp.float32)
        inverse = lax.rsqrt(lax.optimization_barrier(jnp.mean(activations * activations, axis=1, keepdims=True)) + EPSILON)
        normed32 = rounded(activations * inverse * gain32)
        projected = jnp.einsum('td,hced->hcet', normed32, project32).astype(jnp.bfloat16)
        attended = lax.map(attend, (projected[:, 0], projected[:, 1], projected[:, 2]))
        attended32 = attended.astype(jnp.float32)
        result = activations + jnp.einsum('het,hed->td', attended32, output32)
        outputs.append(result.astype(jnp.bfloat16))
        grad_rows = cotangent[index].astype(jnp.float32)
        grad_attended = jnp.einsum('td,hed->het', grad_rows, output32).astype(jnp.bfloat16)
        output_total = output_total + jnp.einsum('het,td->hed', attended32, grad_rows)
        grad_projected = lax.map(backward, (projected[:, 0], projected[:, 1], projected[:, 2], grad_attended))
        grad_projected32 = grad_projected.astype(jnp.float32)
        project_total = project_total + jnp.einsum('hcet,td->hced', grad_projected32, normed32)
        grad_normed = jnp.einsum('hcet,hced->td', grad_projected32, project32)
        scaled = gain32 * grad_normed
        cubed = inverse * inverse * inverse
        grad_activations = inverse * scaled - activations * cubed * lax.optimization_barrier(jnp.mean(activations * scaled, axis=1, keepdims=True))
        gain_total = gain_total + lax.optimization_barrier(jnp.sum(grad_normed * activations * inverse, axis=0))
        grad_features = (grad_rows + grad_activations).astype(jnp.bfloat16)
        map_grads = []
        for shard in range(shards):
            places, usable = unpack_positions(counts[index, shard], slots)
            part = grad_features[shard * TOK_DEV:(shard + 1) * TOK_DEV]
            taken = jnp.take(part, places.reshape(-1), axis=0).reshape(owners, slots, width)
            map_grads.append(jnp.where(usable[..., None], taken, jnp.zeros((), jnp.bfloat16)))
        owner_grads.append(jnp.stack(map_grads, axis=0))
    token_grad = jnp.stack(owner_grads, axis=0).transpose(2, 0, 1, 3, 4)
    onehot = (levels[..., None] == jnp.arange(level_table.shape[0], dtype=jnp.int32)).astype(jnp.float32)
    table_grad = jnp.einsum('omsjl,omsjd->ld', onehot, token_grad.astype(jnp.float32)) * factor
    return (jnp.stack(outputs, axis=0), token_grad, project_total * factor, output_total * factor, gain_total * factor, table_grad)
```

```python
import functools
import math

import jax
import jax.numpy as jnp
from jax import lax
from jax.experimental import pallas as pl
from jax.experimental.pallas import tpu as pltpu
from jax.sharding import PartitionSpec as P

EPSILON = 1e-05
BF16 = jnp.bfloat16
F32 = jnp.float32
MIB = 2**20
LANES = 128


def dot(a, b, ca, cb):
    return lax.dot_general(a, b, (((ca,), (cb,)), ((), ())), preferred_element_type=F32)


def whole(shape):
    zeros = (0,) * len(shape)
    return pl.BlockSpec(shape, lambda i: zeros)


def vmem(mib):
    return pltpu.CompilerParams(vmem_limit_bytes=mib * MIB)


def pack_positions(counts, rows, slots):
    starts = jnp.cumsum(counts) - counts
    place = jnp.arange(rows, dtype=jnp.int32)
    before = (starts[None, :] <= place[:, None]).astype(jnp.int32)
    owner = jnp.sum(before, axis=1) - 1
    first = jnp.max(jnp.where(before > 0, starts[None, :], 0), axis=1)
    return owner * slots + place - first


def project_body(
    received, place, gain, cotangent, weight, out_weight, packed, features, level, normed, heads
):
    rows, width = features.shape

    @pl.when(pl.program_id(0) == 0)
    def _():
        slot = lax.broadcasted_iota(jnp.int32, (rows, received.shape[0]), 1)
        pick = jnp.where(slot == place[...], 1.0, 0.0).astype(BF16)
        taken = dot(pick, received[...], 1, 0)
        active = taken[:, :width]
        features[...] = active.astype(BF16)
        level[...] = taken[:, width:].astype(BF16)
        inverse = lax.rsqrt(jnp.mean(active * active, axis=1, keepdims=True) + EPSILON)
        normed[...] = (active * inverse * gain[...]).astype(BF16)

    size = out_weight.shape[1]
    for h in range(heads):
        packed[h, : 3 * size, :] = dot(weight[h], normed[...], 1, 1).astype(BF16)
        packed[h, 3 * size :, :] = dot(out_weight[h], cotangent[...], 1, 1).astype(BF16)


def project(received, place, gain, cotangent, weight, out_weight):
    rows, width = cotangent.shape
    count, three, _ = weight.shape
    size = out_weight.shape[1]
    heads = 2
    return pl.pallas_call(
        functools.partial(project_body, heads=heads),
        grid=(count // heads,),
        in_specs=[
            whole(received.shape),
            whole((rows, 1)),
            whole((1, width)),
            whole((rows, width)),
            pl.BlockSpec((heads, three, width), lambda i: (i, 0, 0)),
            pl.BlockSpec((heads, size, width), lambda i: (i, 0, 0)),
        ],
        out_specs=[
            pl.BlockSpec((heads, three + size, rows), lambda i: (i, 0, 0)),
            whole((rows, width)),
            whole((rows, LANES)),
            whole((rows, width)),
        ],
        out_shape=[
            jax.ShapeDtypeStruct((count, three + size, rows), BF16),
            jax.ShapeDtypeStruct((rows, width), BF16),
            jax.ShapeDtypeStruct((rows, LANES), BF16),
            jax.ShapeDtypeStruct((rows, width), BF16),
        ],
        compiler_params=vmem(40),
        name="project",
    )(received, place, gain, cotangent, weight, out_weight)


def attend_body(
    packed, out, query, grad, keys, values, key_total, value_total, *, scale, shift, step
):
    shards, four, rows = packed.shape
    size = four // 4
    length = shards * rows
    rate = scale * math.log2(math.e)
    offset = shift * math.log2(math.e)
    for s in range(shards):
        part = slice(s * rows, (s + 1) * rows)
        query[part, :] = jnp.transpose(packed[s, :size, :])
        grad[part, :] = jnp.transpose(packed[s, 3 * size :, :])
        keys[:, part] = packed[s, size : 2 * size, :]
        values[:, part] = packed[s, 2 * size : 3 * size, :]
    key_total[...] = jnp.zeros_like(key_total)
    value_total[...] = jnp.zeros_like(value_total)

    def one_block(i, _):
        mine = pl.ds(pl.multiple_of(i * rows, rows), rows)
        q, g = query[mine, :], grad[mine, :]
        q_across, g_across = packed[i, :size, :], packed[i, 3 * size :, :]

        attended = jnp.zeros((size, rows), F32)
        grad_query = jnp.zeros((size, rows), F32)
        for j in range(length // step):
            part = slice(j * step, (j + 1) * step)
            k, v = keys[:, part], values[:, part]
            odds = jnp.exp2(offset - dot(q, k, 1, 0) * rate)
            probs = pl.reciprocal(1.0 + odds, approx=True)
            weights = probs.astype(BF16)
            slope = probs - probs * probs
            grad_scores = (dot(g, v, 1, 0) * slope).astype(BF16)
            attended = attended + dot(v, weights, 1, 1)
            grad_query = grad_query + dot(k, grad_scores, 1, 1)
            key_total[:, part] += dot(q_across, grad_scores, 1, 0)
            value_total[:, part] += dot(g_across, weights, 1, 0)
        out[i, :size, :] = attended.astype(BF16)
        out[i, size : 2 * size, :] = (grad_query * scale).astype(BF16)
        return 0

    lax.fori_loop(0, shards, one_block, 0)
    for s in range(shards):
        part = slice(s * rows, (s + 1) * rows)
        out[s, 2 * size : 3 * size, :] = (key_total[:, part] * scale).astype(BF16)
        out[s, 3 * size :, :] = value_total[:, part].astype(BF16)


def attend(packed, scale, shift):
    shards, four, rows = packed.shape
    size, length = four // 4, shards * rows
    return pl.pallas_call(
        functools.partial(attend_body, scale=scale, shift=shift, step=min(1024, length)),
        in_specs=[pl.BlockSpec(memory_space=pltpu.VMEM)],
        out_specs=pl.BlockSpec(memory_space=pltpu.VMEM),
        out_shape=jax.ShapeDtypeStruct(packed.shape, BF16),
        scratch_shapes=[
            pltpu.VMEM((length, size), BF16),
            pltpu.VMEM((length, size), BF16),
            pltpu.VMEM((size, length), BF16),
            pltpu.VMEM((size, length), BF16),
            pltpu.VMEM((size, length), F32),
            pltpu.VMEM((size, length), F32),
        ],
        compiler_params=vmem(48),
        cost_estimate=pl.CostEstimate(
            flops=48 * length * length * size, bytes_accessed=8 * length * size, transcendentals=0
        ),
        name="attend",
    )(packed)


def weight_grad_body(mixed, cotangent, normed, out, total, *, factor):
    shard = pl.program_id(0)
    size = mixed.shape[1] // 4

    @pl.when(shard == 0)
    def _():
        total[...] = jnp.zeros_like(total)

    total[:size, :] += dot(mixed[0, :size, :], cotangent[...], 1, 0)
    total[size:, :] += dot(mixed[0, size:, :], normed[...], 1, 0)

    @pl.when(shard == pl.num_programs(0) - 1)
    def _():
        tiles, _, part = out.shape
        for r in range(tiles):
            out[r] = (total[:, r * part : (r + 1) * part] * factor).astype(BF16)


def weight_grad(mixed, cotangent, normed, tiles, factor):
    shards, four, rows = mixed.shape
    width = normed.shape[1]
    shape = (tiles, four, width // tiles)
    return pl.pallas_call(
        functools.partial(weight_grad_body, factor=factor),
        grid=(shards,),
        in_specs=[
            pl.BlockSpec((1, four, rows), lambda i: (i, 0, 0)),
            pl.BlockSpec((rows, width), lambda i: (i, 0)),
            pl.BlockSpec((rows, width), lambda i: (i, 0)),
        ],
        out_specs=whole(shape),
        out_shape=jax.ShapeDtypeStruct(shape, BF16),
        scratch_shapes=[pltpu.VMEM((four, width), F32)],
        compiler_params=vmem(32),
        name="weight_grad",
    )(mixed, cotangent, normed)


def finish_body(
    mixed,
    weight,
    out_weight,
    features,
    normed_gain,
    cotangent,
    level,
    place,
    output,
    outgoing,
    small,
    out_total,
    grad_total,
    *,
    heads,
    factor,
):
    size = out_weight.shape[1]
    index = pl.program_id(0)

    @pl.when(index == 0)
    def _():
        out_total[...] = jnp.zeros_like(out_total)
        grad_total[...] = jnp.zeros_like(grad_total)

    attended = jnp.concatenate([mixed[h, :size, :] for h in range(heads)], axis=0)
    grads = jnp.concatenate([mixed[h, size:, :] for h in range(heads)], axis=0)
    out_total[...] += dot(attended, out_weight[...].reshape(heads * size, -1), 0, 0)
    grad_total[...] += dot(grads, weight[...].reshape(heads * 3 * size, -1), 0, 0)

    @pl.when(index == pl.num_programs(0) - 1)
    def _():
        rows, _ = features.shape
        active = features[...].astype(F32)
        output[...] = (active + out_total[...]).astype(BF16)
        inverse = lax.rsqrt(jnp.mean(active * active, axis=1, keepdims=True) + EPSILON)
        grad_normed = grad_total[...]
        scaled = normed_gain[...] * grad_normed
        cubed = inverse * inverse * inverse
        grad_active = inverse * scaled - active * cubed * jnp.mean(
            active * scaled, axis=1, keepdims=True
        )
        grad_features = (cotangent[...].astype(F32) + grad_active).astype(BF16)
        slot = lax.broadcasted_iota(jnp.int32, (outgoing.shape[0], rows), 0)
        pick = jnp.where(slot == place[...], 1.0, 0.0).astype(BF16)
        outgoing[...] = dot(pick, grad_features, 1, 0).astype(BF16)
        table = dot(level[...], grad_features, 0, 0)
        gain = jnp.sum(grad_normed * active * inverse, axis=0, keepdims=True)
        line = lax.broadcasted_iota(jnp.int32, small.shape, 0)
        small[...] = jnp.where(line == small.shape[0] - 1, gain, table[: small.shape[0]]) * factor


def finish(mixed, weight, out_weight, features, gain, cotangent, level, place, slots, factor):
    count, four, rows = mixed.shape
    width = features.shape[1]
    size = four // 4
    heads = 4
    return pl.pallas_call(
        functools.partial(finish_body, heads=heads, factor=factor),
        grid=(count // heads,),
        in_specs=[
            pl.BlockSpec((heads, four, rows), lambda i: (i, 0, 0)),
            pl.BlockSpec((heads, 3 * size, width), lambda i: (i, 0, 0)),
            pl.BlockSpec((heads, size, width), lambda i: (i, 0, 0)),
            whole((rows, width)),
            whole((1, width)),
            whole((rows, width)),
            whole((rows, LANES)),
            whole((1, rows)),
        ],
        out_specs=[whole((rows, width)), whole((slots, width)), whole((8, width))],
        out_shape=[
            jax.ShapeDtypeStruct((rows, width), BF16),
            jax.ShapeDtypeStruct((slots, width), BF16),
            jax.ShapeDtypeStruct((8, width), F32),
        ],
        scratch_shapes=[pltpu.VMEM((rows, width), F32), pltpu.VMEM((rows, width), F32)],
        compiler_params=vmem(40),
        name="finish",
    )(mixed, weight, out_weight, features, gain, cotangent, level, place)


def sum_all(value, axes):
    for axis in axes:
        count = lax.axis_size(axis)
        reach = 1
        while reach < count:
            value = value + lax.ppermute(value, axis, [(i, i ^ reach) for i in range(count)])
            reach *= 2
    return value


def on_device(
    tokens, levels, counts, level_table, norm_gain, project_weight, output_weight, cotangent
):
    tiles = lax.axis_size("tile")
    shards = lax.axis_size("seq")
    tile_index = lax.axis_index("tile")
    shard_index = lax.axis_index("seq")
    owners = tiles * shards
    slots = tokens.shape[3]
    width = tokens.shape[4]
    rows = cotangent.shape[1]
    length = rows * shards
    count, _, size, _ = project_weight.shape
    scale = 1.0 / math.sqrt(size)
    shift = math.log(length)
    factor = 1.0 / math.sqrt(tiles * length)
    kinds = level_table.shape[0]

    grad_rows = cotangent[0]
    all_grad_rows = lax.all_gather(grad_rows, "seq", tiled=True)

    me = tile_index * shards + shard_index
    my_counts = lax.dynamic_index_in_dim(counts, me, 2, keepdims=False)
    used = jnp.arange(slots, dtype=jnp.int32) < my_counts[..., None]
    onehot = (levels[0][..., None] == jnp.arange(LANES, dtype=jnp.int32)).astype(BF16)
    embedded = tokens[0].astype(F32) + jnp.einsum(
        "msjl,ld->msjd", onehot[..., :kinds], level_table, preferred_element_type=F32
    )
    embedded = jnp.concatenate([embedded.astype(BF16), onehot], axis=-1)
    embedded = jnp.where(used[..., None], embedded, jnp.zeros((), BF16))
    received = lax.all_to_all(
        embedded.reshape(owners, slots, width + LANES),
        ("tile", "seq"),
        split_axis=0,
        concat_axis=0,
        tiled=True,
    )
    map_counts = lax.dynamic_index_in_dim(counts, tile_index, 0, keepdims=False)
    own_counts = lax.dynamic_index_in_dim(map_counts, shard_index, 0, keepdims=False)
    place = pack_positions(own_counts, rows, slots)
    gain = norm_gain.reshape(1, width)
    weight = project_weight.reshape(count, 3 * size, width)

    packed, features, level, normed = project(
        received.reshape(owners * slots, width + LANES),
        place.reshape(rows, 1),
        gain,
        grad_rows,
        weight,
        output_weight,
    )
    by_head = lax.all_to_all(packed, "seq", split_axis=0, concat_axis=0, tiled=True)
    all_normed = lax.all_gather(normed, "seq", tiled=True)
    attended = attend(by_head, scale, shift)
    mixed = lax.all_to_all(attended, "seq", split_axis=0, concat_axis=0, tiled=True)
    shares = weight_grad(attended, all_grad_rows, all_normed, tiles, factor)
    output, outgoing, small = finish(
        mixed,
        weight,
        output_weight,
        features,
        gain,
        grad_rows,
        level,
        place.reshape(1, rows),
        owners * slots,
        factor,
    )
    returned = lax.all_to_all(
        outgoing.reshape(owners, slots, width),
        ("tile", "seq"),
        split_axis=0,
        concat_axis=0,
        tiled=True,
    )
    token_grad = returned.reshape(tiles, shards, slots, width)
    shares = lax.all_to_all(shares, "tile", split_axis=0, concat_axis=0, tiled=True)
    shares = jnp.sum(shares.astype(F32), axis=0)
    small = sum_all(small, ("tile", "seq"))
    return (
        output[None],
        token_grad[None],
        shares[size:].reshape(1, 3, size, width // tiles),
        shares[:size].reshape(1, size, width // tiles),
        small[7],
        small[:kinds],
    )


def solution(mesh):
    return jax.shard_map(
        on_device,
        mesh=mesh,
        in_specs=(
            P(("tile", "seq"), None, None, None, None),
            P(("tile", "seq"), None, None, None),
            P(),
            P(),
            P(),
            P(),
            P(),
            P("tile", "seq", None),
        ),
        out_specs=(
            P("tile", "seq", None),
            P(("tile", "seq"), None, None, None, None),
            P("seq", None, None, "tile"),
            P("seq", None, "tile"),
            P(),
            P(),
        ),
        check_vma=False,
    )
```

```python
import functools
import math

import jax
import jax.numpy as jnp
from jax import lax
from jax.experimental import pallas as pl
from jax.experimental.pallas import tpu as pltpu
from jax.sharding import PartitionSpec as P

EPSILON = 1e-05
BF16 = jnp.bfloat16
F32 = jnp.float32
MIB = 2**20
LANES = 128
LINES = 8


def dot(a, b, ca, cb):
    return lax.dot_general(a, b, (((ca,), (cb,)), ((), ())), preferred_element_type=F32)


def whole(shape):
    zeros = (0,) * len(shape)
    return pl.BlockSpec(shape, lambda i: zeros)


def vmem(mib):
    return pltpu.CompilerParams(vmem_limit_bytes=mib * MIB)


def pack_positions(counts, rows, slots):
    starts = jnp.cumsum(counts) - counts
    place = jnp.arange(rows, dtype=jnp.int32)
    before = (starts[None, :] <= place[:, None]).astype(jnp.int32)
    owner = jnp.sum(before, axis=1) - 1
    first = jnp.max(jnp.where(before > 0, starts[None, :], 0), axis=1)
    return owner * slots + place - first


def project_body(
    received, place, gain, cotangent, weight, out_weight, packed, features, normed, local, heads
):
    rows, width = features.shape

    @pl.when(pl.program_id(0) == 0)
    def _():
        slot = lax.broadcasted_iota(jnp.int32, (rows, received.shape[0]), 1)
        pick = jnp.where(slot == place[...], 1.0, 0.0).astype(BF16)
        taken = dot(pick, received[...], 1, 0)
        active = taken[:, :width]
        features[...] = active.astype(BF16)
        level = taken[:, width:]
        inverse = lax.rsqrt(jnp.mean(active * active, axis=1, keepdims=True) + EPSILON)
        normed[:rows, :] = (active * inverse * gain[...]).astype(BF16)
        kept = jnp.transpose(level * inverse)[:LINES]
        kept = jnp.concatenate([kept, kept - kept.astype(BF16).astype(F32)], axis=0)
        normed[rows:, :rows] = kept.astype(BF16)
        normed[rows:, rows:] = jnp.zeros((2 * LINES, width - rows), BF16)
        local[...] = dot(level.astype(BF16), cotangent[...], 0, 0)[:LINES]

    size = out_weight.shape[1]
    rows, width = features.shape
    projected = dot(weight[...].reshape(heads * 3 * size, width), normed[:rows, :], 1, 1)
    grads = dot(out_weight[...].reshape(heads * size, width), cotangent[...], 1, 1)
    packed[:, : 3 * size, :] = projected.astype(BF16).reshape(heads, 3 * size, rows)
    packed[:, 3 * size :, :] = grads.astype(BF16).reshape(heads, size, rows)


def project(received, place, gain, cotangent, weight, out_weight):
    rows, width = cotangent.shape
    count, three, _ = weight.shape
    size = out_weight.shape[1]
    heads = 4
    return pl.pallas_call(
        functools.partial(project_body, heads=heads),
        grid=(count // heads,),
        in_specs=[
            whole(received.shape),
            whole((rows, 1)),
            whole((1, width)),
            whole((rows, width)),
            pl.BlockSpec((heads, three, width), lambda i: (i, 0, 0)),
            pl.BlockSpec((heads, size, width), lambda i: (i, 0, 0)),
        ],
        out_specs=[
            pl.BlockSpec((heads, three + size, rows), lambda i: (i, 0, 0)),
            whole((rows, width)),
            whole((rows + 2 * LINES, width)),
            whole((LINES, width)),
        ],
        out_shape=[
            jax.ShapeDtypeStruct((count, three + size, rows), BF16),
            jax.ShapeDtypeStruct((rows, width), BF16),
            jax.ShapeDtypeStruct((rows + 2 * LINES, width), BF16),
            jax.ShapeDtypeStruct((LINES, width), F32),
        ],
        compiler_params=vmem(60),
        name="project",
    )(received, place, gain, cotangent, weight, out_weight)


def attend_body(
    packed, out, query, grad, keys, values, key_total, value_total, *, scale, shift, step
):
    shards, four, rows = packed.shape
    size = four // 4
    length = shards * rows
    rate = scale * math.log2(math.e)
    offset = shift * math.log2(math.e)
    for s in range(shards):
        part = slice(s * rows, (s + 1) * rows)
        query[part, :] = jnp.transpose(packed[s, :size, :])
        grad[part, :] = jnp.transpose(packed[s, 3 * size :, :])
        keys[:, part] = packed[s, size : 2 * size, :]
        values[:, part] = packed[s, 2 * size : 3 * size, :]
    key_total[...] = jnp.zeros_like(key_total)
    value_total[...] = jnp.zeros_like(value_total)

    def one_block(i, _):
        mine = pl.ds(pl.multiple_of(i * rows, rows), rows)
        q, g = query[mine, :], grad[mine, :]
        q_across, g_across = packed[i, :size, :], packed[i, 3 * size :, :]

        attended = jnp.zeros((size, rows), F32)
        grad_query = jnp.zeros((size, rows), F32)
        for j in range(length // step):
            part = slice(j * step, (j + 1) * step)
            k, v = keys[:, part], values[:, part]
            odds = jnp.exp2(offset - dot(q, k, 1, 0) * rate)
            probs = pl.reciprocal(1.0 + odds, approx=True)
            weights = probs.astype(BF16)
            slope = probs - probs * probs
            grad_scores = (dot(g, v, 1, 0) * slope).astype(BF16)
            attended = attended + dot(v, weights, 1, 1)
            grad_query = grad_query + dot(k, grad_scores, 1, 1)
            key_total[:, part] += dot(q_across, grad_scores, 1, 0)
            value_total[:, part] += dot(g_across, weights, 1, 0)
        out[i, :size, :] = attended.astype(BF16)
        out[i, size : 2 * size, :] = (grad_query * scale).astype(BF16)
        return 0

    lax.fori_loop(0, shards, one_block, 0)
    for s in range(shards):
        part = slice(s * rows, (s + 1) * rows)
        out[s, 2 * size : 3 * size, :] = (key_total[:, part] * scale).astype(BF16)
        out[s, 3 * size :, :] = value_total[:, part].astype(BF16)


def attend(packed, scale, shift):
    shards, four, rows = packed.shape
    size, length = four // 4, shards * rows
    return pl.pallas_call(
        functools.partial(attend_body, scale=scale, shift=shift, step=min(1024, length)),
        in_specs=[pl.BlockSpec(memory_space=pltpu.VMEM)],
        out_specs=pl.BlockSpec(memory_space=pltpu.VMEM),
        out_shape=jax.ShapeDtypeStruct(packed.shape, BF16),
        scratch_shapes=[
            pltpu.VMEM((length, size), BF16),
            pltpu.VMEM((length, size), BF16),
            pltpu.VMEM((size, length), BF16),
            pltpu.VMEM((size, length), BF16),
            pltpu.VMEM((size, length), F32),
            pltpu.VMEM((size, length), F32),
        ],
        compiler_params=vmem(48),
        cost_estimate=pl.CostEstimate(
            flops=48 * length * length * size, bytes_accessed=8 * length * size, transcendentals=0
        ),
        name="attend",
    )(packed)


def weight_grad_body(
    head,
    mixed,
    projected,
    normed,
    weight,
    gain,
    local,
    out,
    attended,
    small,
    total,
    by_level,
    *,
    factor,
):
    del head
    step = pl.program_id(0)
    rows = mixed.shape[2]
    first = mixed.shape[1] // 4
    width = normed.shape[2]

    @pl.when(step == 0)
    def _():
        total[...] = jnp.zeros_like(total)
        by_level[...] = jnp.zeros_like(by_level)

    attended[...] = mixed[:, :first, :]
    for s in range(mixed.shape[0]):
        grads = mixed[s, first:, :]
        features = normed[s, :rows, :]
        level = normed[s, rows:, :rows].astype(F32)
        level = level[:LINES] + level[LINES:]
        by_level[...] += dot(level.astype(BF16), grads, 1, 1)
        along = jnp.sum(
            grads.astype(F32) * projected[s, : 3 * first, :].astype(F32), axis=0, keepdims=True
        )
        drift = level * (along * (1.0 / width))
        drift = jnp.concatenate([drift, jnp.zeros_like(drift)], axis=0).astype(BF16)
        total[...] += dot(jnp.concatenate([grads, drift], axis=0), features, 1, 0)

    @pl.when(step == pl.num_programs(0) - 1)
    def _():
        tiles, _, part = out.shape
        for r in range(tiles):
            out[r] = (total[: 3 * first, r * part : (r + 1) * part] * factor).astype(BF16)
        scale = gain[...]
        drift = total[3 * first : 3 * first + LINES, :] / scale
        table = dot(by_level[...].astype(BF16), weight[0], 1, 0) * scale - drift
        table = table + local[...]
        for_gain = weight[0].astype(F32) * total[: 3 * first, :]
        for_gain = jnp.sum(for_gain, axis=0, keepdims=True) / scale
        line = lax.broadcasted_iota(jnp.int32, table.shape, 0)
        both = jnp.where(line == LINES - 1, for_gain, table) * factor
        for c in range(width // LANES):
            small[c * LINES : (c + 1) * LINES, :] = both[:, c * LANES : (c + 1) * LANES]


def weight_grad(head, mixed, projected, normed, weight, gain, local, tiles, factor):
    shards, four, rows = mixed.shape
    width = normed.shape[-1]
    first = four // 4
    lines = four - first
    each = 2
    shape = (tiles, lines, width // tiles)
    small = (width // LANES * LINES, LANES)

    def by_step(shape):
        return pl.BlockSpec((each,) + shape[1:], lambda i, h: (i, 0, 0))

    def fixed(shape):
        zeros = (0,) * len(shape)
        return pl.BlockSpec(shape, lambda i, h: zeros)

    return pl.pallas_call(
        functools.partial(weight_grad_body, factor=factor),
        grid_spec=pltpu.PrefetchScalarGridSpec(
            num_scalar_prefetch=1,
            grid=(shards // each,),
            in_specs=[by_step(part.shape) for part in (mixed, projected, normed)]
            + [
                pl.BlockSpec((1, lines, width), lambda i, h: (h[0], 0, 0)),
                fixed(gain.shape),
                fixed(local.shape),
            ],
            out_specs=[fixed(shape), by_step((shards, first, rows)), fixed(small)],
            scratch_shapes=[
                pltpu.VMEM((lines + 2 * LINES, width), F32),
                pltpu.VMEM((LINES, lines), F32),
            ],
        ),
        out_shape=[
            jax.ShapeDtypeStruct(shape, BF16),
            jax.ShapeDtypeStruct((shards, first, rows), BF16),
            jax.ShapeDtypeStruct(small, F32),
        ],
        compiler_params=vmem(60),
        cost_estimate=pl.CostEstimate(flops=1, bytes_accessed=1, transcendentals=0),
        name="weight_grad",
    )(head, mixed, projected, normed, weight, gain, local)


def out_grad_body(column, small, *refs, factor):
    out = refs[-1]
    ways = out.shape[0]
    attended, cotangents = refs[:ways], refs[ways : 2 * ways]
    shards, size, _ = attended[0].shape
    total = 0.0
    for k, cotangent in enumerate(cotangents):
        s = (column[0] + shards - k) % shards
        rows = jnp.concatenate([part[s] for part in attended], axis=0)
        total = total + dot(rows, cotangent[...], 1, 0)
    total = (total * factor).astype(BF16)
    tiles = total.shape[1] // LANES
    high = small[...].astype(BF16)
    low = (small[...] - high.astype(F32)).astype(BF16)
    for h in range(ways):
        for r in range(tiles):
            out[h, r * size : (r + 1) * size, :] = total[
                h * size : (h + 1) * size, r * LANES : (r + 1) * LANES
            ]
        out[h, tiles * size : tiles * size + high.shape[0], :] = high
        out[h, tiles * size + high.shape[0] :, :] = low


def out_grad(column, small, attended, cotangents, factor):
    _, size, _ = attended[0].shape
    tiles = cotangents[0].shape[-1] // LANES
    shape = (len(attended), tiles * size + 2 * small.shape[0], LANES)
    return pl.pallas_call(
        functools.partial(out_grad_body, factor=factor),
        in_specs=[pl.BlockSpec(memory_space=pltpu.SMEM)]
        + [pl.BlockSpec(memory_space=pltpu.VMEM)] * (1 + len(attended) + len(cotangents)),
        out_specs=pl.BlockSpec(memory_space=pltpu.VMEM),
        out_shape=jax.ShapeDtypeStruct(shape, BF16),
        compiler_params=vmem(48),
        cost_estimate=pl.CostEstimate(flops=1, bytes_accessed=1, transcendentals=0),
        name="out_grad",
    )(column, small, *attended, *cotangents)


def finish_body(
    mixed,
    weight,
    out_weight,
    features,
    normed_gain,
    cotangent,
    place,
    output,
    outgoing,
    out_total,
    grad_total,
    *,
    heads,
):
    size = out_weight.shape[1]
    index = pl.program_id(0)

    @pl.when(index == 0)
    def _():
        out_total[...] = jnp.zeros_like(out_total)
        grad_total[...] = jnp.zeros_like(grad_total)

    attended = jnp.concatenate([mixed[h, :size, :] for h in range(heads)], axis=0)
    grads = jnp.concatenate([mixed[h, size:, :] for h in range(heads)], axis=0)
    out_total[...] += dot(attended, out_weight[...].reshape(heads * size, -1), 0, 0)
    grad_total[...] += dot(grads, weight[...].reshape(heads * 3 * size, -1), 0, 0)

    @pl.when(index == pl.num_programs(0) - 1)
    def _():
        rows, _ = features.shape
        active = features[...].astype(F32)
        output[...] = (active + out_total[...]).astype(BF16)
        inverse = lax.rsqrt(jnp.mean(active * active, axis=1, keepdims=True) + EPSILON)
        grad_normed = grad_total[...]
        scaled = normed_gain[...] * grad_normed
        cubed = inverse * inverse * inverse
        grad_active = inverse * scaled - active * cubed * jnp.mean(
            active * scaled, axis=1, keepdims=True
        )
        grad_features = (cotangent[...].astype(F32) + grad_active).astype(BF16)
        slot = lax.broadcasted_iota(jnp.int32, (outgoing.shape[0], rows), 0)
        pick = jnp.where(slot == place[...], 1.0, 0.0).astype(BF16)
        outgoing[...] = dot(pick, grad_features, 1, 0).astype(BF16)


def finish(mixed, weight, out_weight, features, gain, cotangent, place, slots):
    count, four, rows = mixed.shape
    width = features.shape[1]
    size = four // 4
    heads = 4
    return pl.pallas_call(
        functools.partial(finish_body, heads=heads),
        grid=(count // heads,),
        in_specs=[
            pl.BlockSpec((heads, four, rows), lambda i: (i, 0, 0)),
            pl.BlockSpec((heads, 3 * size, width), lambda i: (i, 0, 0)),
            pl.BlockSpec((heads, size, width), lambda i: (i, 0, 0)),
            whole((rows, width)),
            whole((1, width)),
            whole((rows, width)),
            whole((1, rows)),
        ],
        out_specs=[whole((rows, width)), whole((slots, width))],
        out_shape=[
            jax.ShapeDtypeStruct((rows, width), BF16),
            jax.ShapeDtypeStruct((slots, width), BF16),
        ],
        scratch_shapes=[pltpu.VMEM((rows, width), F32), pltpu.VMEM((rows, width), F32)],
        compiler_params=vmem(60),
        name="finish",
    )(mixed, weight, out_weight, features, gain, cotangent, place)


def pick(value, k, axis=0):
    return lax.dynamic_index_in_dim(value, k, axis, keepdims=False)


def sum_to_tiles(value, small, tile_index):
    tiles, lines, lanes = value.shape
    ways = tiles // 2
    core, place = tile_index % 2, tile_index // 2
    value = value.reshape(ways, 2, lines, lanes)

    def mine(k):
        return pick(value, k, 1).reshape(ways * lines, lanes)

    other = jnp.concatenate([mine(1 - core), small], axis=0)
    other = lax.ppermute(other, "tile", [(i, i ^ 1) for i in range(tiles)])
    both = jnp.concatenate([mine(core), small], axis=0) + other
    value, small = both[: ways * lines].reshape(ways, lines, lanes), both[ways * lines :]
    parts = [jnp.concatenate([pick(value, place), small], axis=0)] + [
        lax.ppermute(
            jnp.concatenate([pick(value, (place + k) % ways), small], axis=0),
            "tile",
            [(i, (i + 2 * k) % tiles) for i in range(tiles)],
        )
        for k in range(1, ways)
    ]
    both = sum(parts[1:], parts[0])
    return both[:lines], both[lines:]


def on_device(
    tokens, levels, counts, level_table, norm_gain, project_weight, output_weight, cotangent
):
    tiles = lax.axis_size("tile")
    shards = lax.axis_size("seq")
    tile_index = lax.axis_index("tile")
    shard_index = lax.axis_index("seq")
    owners = tiles * shards
    slots = tokens.shape[3]
    width = tokens.shape[4]
    rows = cotangent.shape[1]
    length = rows * shards
    count, _, size, _ = project_weight.shape
    scale = 1.0 / math.sqrt(size)
    shift = math.log(length)
    factor = 1.0 / math.sqrt(tiles * length)
    kinds = level_table.shape[0]

    grad_rows = cotangent[0]
    side = math.isqrt(shards)
    line, column = shard_index // side, shard_index % side

    def along_line(value, k):
        return lax.ppermute(
            value, "seq", [(i, i // side * side + (i + k) % side) for i in range(shards)]
        )

    def along_column(value, k):
        return lax.ppermute(value, "seq", [(i, (i + k * side) % shards) for i in range(shards)])

    me = tile_index * shards + shard_index
    my_counts = lax.dynamic_index_in_dim(counts, me, 2, keepdims=False)
    used = jnp.arange(slots, dtype=jnp.int32) < my_counts[..., None]
    onehot = (levels[0][..., None] == jnp.arange(LANES, dtype=jnp.int32)).astype(BF16)
    embedded = tokens[0].astype(F32) + jnp.einsum(
        "msjl,ld->msjd", onehot[..., :kinds], level_table, preferred_element_type=F32
    )
    embedded = jnp.concatenate([embedded.astype(BF16), onehot], axis=-1)
    embedded = jnp.where(used[..., None], embedded, jnp.zeros((), BF16))
    received = lax.all_to_all(
        embedded.reshape(owners, slots, width + LANES),
        ("tile", "seq"),
        split_axis=0,
        concat_axis=0,
        tiled=True,
    )
    map_counts = lax.dynamic_index_in_dim(counts, tile_index, 0, keepdims=False)
    own_counts = lax.dynamic_index_in_dim(map_counts, shard_index, 0, keepdims=False)
    place = pack_positions(own_counts, rows, slots)
    gain = norm_gain.reshape(1, width)
    weight = project_weight.reshape(count, 3 * size, width)

    packed, features, normed, local = project(
        received.reshape(owners * slots, width + LANES),
        place.reshape(rows, 1),
        gain,
        grad_rows,
        weight,
        output_weight,
    )
    by_head = lax.all_to_all(packed, "seq", split_axis=0, concat_axis=0, tiled=True)
    all_normed = lax.all_gather(normed, "seq")
    by_head, line_rows = lax.optimization_barrier((by_head, grad_rows))
    line_rows = [line_rows] + [along_line(line_rows, k) for k in range(1, side)]
    attended = attend(by_head, scale, shift)
    attended, line_rows = lax.optimization_barrier((attended, line_rows))
    mixed = lax.all_to_all(attended, "seq", split_axis=0, concat_axis=0, tiled=True)

    shares, head_attended, small = weight_grad(
        shard_index.reshape(1),
        attended,
        by_head,
        all_normed,
        weight,
        gain,
        local,
        tiles,
        factor,
    )
    head_attended = head_attended.reshape(side, side, size, rows)
    column_attended = [pick(head_attended, line)] + [
        along_column(pick(head_attended, (line + k) % side), k) for k in range(1, side)
    ]
    out_shares = out_grad(column.reshape(1), small, column_attended, line_rows, factor)
    out_shares = sum(
        [along_column(out_shares[k], -k).astype(F32) for k in range(1, side)],
        out_shares[0].astype(F32),
    )
    mixed, out_shares, shares = lax.optimization_barrier((mixed, out_shares, shares))
    output, outgoing = finish(
        mixed,
        weight,
        output_weight,
        features,
        gain,
        grad_rows,
        place.reshape(1, rows),
        owners * slots,
    )
    returned = lax.all_to_all(
        outgoing.reshape(owners, slots, width),
        ("tile", "seq"),
        split_axis=0,
        concat_axis=0,
        tiled=True,
    )
    token_grad = returned.reshape(tiles, shards, slots, width)
    lines = tiles * size
    small_lines = (out_shares.shape[0] - lines) // 2
    small = out_shares[lines : lines + small_lines] + out_shares[lines + small_lines :]
    out_shares = out_shares[:lines].reshape(tiles, size, LANES)
    shares = jnp.concatenate([out_shares, shares.astype(F32)], axis=1)
    shares, small = sum_to_tiles(shares, small, tile_index)
    small = sum([along_line(small, k) for k in range(1, side)], small)
    small = small.reshape(width // LANES, LINES, LANES).transpose(1, 0, 2).reshape(LINES, width)
    return (
        output[None],
        token_grad[None],
        shares[size:].reshape(1, 3, size, width // tiles),
        shares[:size].reshape(1, size, width // tiles),
        small[LINES - 1],
        small[:kinds],
    )


def solution(mesh):
    return jax.shard_map(
        on_device,
        mesh=mesh,
        in_specs=(
            P(("tile", "seq"), None, None, None, None),
            P(("tile", "seq"), None, None, None),
            P(),
            P(),
            P(),
            P(),
            P(),
            P("tile", "seq", None),
        ),
        out_specs=(
            P("tile", "seq", None),
            P(("tile", "seq"), None, None, None, None),
            P("seq", None, None, "tile"),
            P("seq", None, "tile"),
            P(),
            P(),
        ),
        check_vma=False,
    )
```

```python
import functools
import math

import jax
import jax.numpy as jnp
from jax import lax
from jax.experimental import pallas as pl
from jax.experimental.pallas import tpu as pltpu
from jax.sharding import PartitionSpec as P

EPSILON = 1e-05
BF16 = jnp.bfloat16
F32 = jnp.float32
MIB = 2**20
LANES = 128
LINES = 8


def dot(a, b, ca, cb):
    return lax.dot_general(a, b, (((ca,), (cb,)), ((), ())), preferred_element_type=F32)


def whole(shape):
    zeros = (0,) * len(shape)
    return pl.BlockSpec(shape, lambda i: zeros)


def vmem(mib):
    return pltpu.CompilerParams(vmem_limit_bytes=mib * MIB)


def pack_positions(counts, rows, slots):
    starts = jnp.cumsum(counts) - counts
    place = jnp.arange(rows, dtype=jnp.int32)
    before = (starts[None, :] <= place[:, None]).astype(jnp.int32)
    owner = jnp.sum(before, axis=1) - 1
    first = jnp.max(jnp.where(before > 0, starts[None, :], 0), axis=1)
    return owner * slots + place - first


def project_body(
    received, place, gain, cotangent, weight, grads, packed, features, normed, local, heads
):
    rows, width = features.shape

    @pl.when(pl.program_id(0) == 0)
    def _():
        count = received.shape[0] * received.shape[1]
        slot = lax.broadcasted_iota(jnp.int32, (rows, count), 1)
        pick = jnp.where(slot == place[...], 1.0, 0.0).astype(BF16)
        taken = dot(pick, received[...].reshape(count, received.shape[2]), 1, 0)
        active = taken[:, :width]
        features[...] = active.astype(BF16)
        level = taken[:, width:]
        inverse = lax.rsqrt(jnp.mean(active * active, axis=1, keepdims=True) + EPSILON)
        normed[:rows, :] = (active * inverse * gain[...]).astype(BF16)
        kept = jnp.transpose(level * inverse)[:LINES]
        kept = jnp.concatenate([kept, kept - kept.astype(BF16).astype(F32)], axis=0)
        normed[rows:, :rows] = kept.astype(BF16)
        normed[rows:, rows:] = jnp.zeros((2 * LINES, width - rows), BF16)
        local[...] = dot(level.astype(BF16), cotangent[...], 0, 0)[:LINES]

    size = grads.shape[1]
    rows, width = features.shape
    projected = dot(weight[...].reshape(heads * 3 * size, width), normed[:rows, :], 1, 1)
    packed[:, : 3 * size, :] = projected.astype(BF16).reshape(heads, 3 * size, rows)
    packed[:, 3 * size :, :] = grads[...]


def project_grads_body(cotangent, weight, out):
    heads, size, rows = out.shape
    grads = dot(weight[...].reshape(heads * size, -1), cotangent[...], 1, 1)
    out[...] = grads.astype(BF16).reshape(heads, size, rows)


def project_grads(cotangent, weight):
    rows, width = cotangent.shape
    count, size, _ = weight.shape
    heads = 4
    return pl.pallas_call(
        project_grads_body,
        grid=(count // heads,),
        in_specs=[
            whole((rows, width)),
            pl.BlockSpec((heads, size, width), lambda i: (i, 0, 0)),
        ],
        out_specs=pl.BlockSpec((heads, size, rows), lambda i: (i, 0, 0)),
        out_shape=jax.ShapeDtypeStruct((count, size, rows), BF16),
        compiler_params=vmem(60),
        name="project_grads",
    )(cotangent, weight)


def project(received, place, gain, cotangent, weight, grads):
    rows, width = cotangent.shape
    count, three, _ = weight.shape
    size = grads.shape[1]
    heads = 4
    return pl.pallas_call(
        functools.partial(project_body, heads=heads),
        grid=(count // heads,),
        in_specs=[
            whole(received.shape),
            whole((rows, 1)),
            whole((1, width)),
            whole((rows, width)),
            pl.BlockSpec((heads, three, width), lambda i: (i, 0, 0)),
            pl.BlockSpec((heads, size, rows), lambda i: (i, 0, 0)),
        ],
        out_specs=[
            pl.BlockSpec((heads, three + size, rows), lambda i: (i, 0, 0)),
            whole((rows, width)),
            whole((rows + 2 * LINES, width)),
            whole((LINES, width)),
        ],
        out_shape=[
            jax.ShapeDtypeStruct((count, three + size, rows), BF16),
            jax.ShapeDtypeStruct((rows, width), BF16),
            jax.ShapeDtypeStruct((rows + 2 * LINES, width), BF16),
            jax.ShapeDtypeStruct((LINES, width), F32),
        ],
        compiler_params=vmem(60),
        name="project",
    )(received, place, gain, cotangent, weight, grads)


def attend_body(
    packed, out, only, query, grad, keys, values, key_total, value_total, *, scale, shift, step
):
    shards, four, rows = packed.shape
    size = four // 4
    length = shards * rows
    rate = scale * math.log2(math.e)
    offset = shift * math.log2(math.e)
    for s in range(shards):
        part = slice(s * rows, (s + 1) * rows)
        query[part, :] = jnp.transpose(packed[s, :size, :])
        grad[part, :] = jnp.transpose(packed[s, 3 * size :, :])
        keys[:, part] = packed[s, size : 2 * size, :]
        values[:, part] = packed[s, 2 * size : 3 * size, :]
    key_total[...] = jnp.zeros_like(key_total)
    value_total[...] = jnp.zeros_like(value_total)

    def one_block(i, _):
        mine = pl.ds(pl.multiple_of(i * rows, rows), rows)
        q, g = query[mine, :], grad[mine, :]
        q_across, g_across = packed[i, :size, :], packed[i, 3 * size :, :]

        attended = jnp.zeros((size, rows), F32)
        grad_query = jnp.zeros((size, rows), F32)
        for j in range(length // step):
            part = slice(j * step, (j + 1) * step)
            k, v = keys[:, part], values[:, part]
            odds = jnp.exp2(offset - dot(q, k, 1, 0) * rate)
            probs = pl.reciprocal(1.0 + odds, approx=True)
            weights = probs.astype(BF16)
            slope = probs - probs * probs
            grad_scores = (dot(g, v, 1, 0) * slope).astype(BF16)
            attended = attended + dot(v, weights, 1, 1)
            grad_query = grad_query + dot(k, grad_scores, 1, 1)
            key_total[:, part] += dot(q_across, grad_scores, 1, 0)
            value_total[:, part] += dot(g_across, weights, 1, 0)
        out[i, :size, :] = attended.astype(BF16)
        only[i] = attended.astype(BF16)
        out[i, size : 2 * size, :] = (grad_query * scale).astype(BF16)
        return 0

    lax.fori_loop(0, shards, one_block, 0)
    for s in range(shards):
        part = slice(s * rows, (s + 1) * rows)
        out[s, 2 * size : 3 * size, :] = (key_total[:, part] * scale).astype(BF16)
        out[s, 3 * size :, :] = value_total[:, part].astype(BF16)


def attend(packed, scale, shift):
    shards, four, rows = packed.shape
    size, length = four // 4, shards * rows
    return pl.pallas_call(
        functools.partial(attend_body, scale=scale, shift=shift, step=min(1024, length)),
        in_specs=[pl.BlockSpec(memory_space=pltpu.VMEM)],
        out_specs=[pl.BlockSpec(memory_space=pltpu.VMEM)] * 2,
        out_shape=[
            jax.ShapeDtypeStruct(packed.shape, BF16),
            jax.ShapeDtypeStruct((shards, size, rows), BF16),
        ],
        scratch_shapes=[
            pltpu.VMEM((length, size), BF16),
            pltpu.VMEM((length, size), BF16),
            pltpu.VMEM((size, length), BF16),
            pltpu.VMEM((size, length), BF16),
            pltpu.VMEM((size, length), F32),
            pltpu.VMEM((size, length), F32),
        ],
        compiler_params=vmem(60),
        cost_estimate=pl.CostEstimate(
            flops=48 * length * length * size, bytes_accessed=8 * length * size, transcendentals=0
        ),
        name="attend",
    )(packed)


def weight_grad_body(
    head,
    mixed,
    projected,
    normed,
    weight,
    gain,
    local,
    out,
    small,
    total,
    by_level,
    *,
    factor,
):
    del head
    step = pl.program_id(0)
    rows = mixed.shape[2]
    first = mixed.shape[1] // 4
    width = normed.shape[2]

    @pl.when(step == 0)
    def _():
        total[...] = jnp.zeros_like(total)
        by_level[...] = jnp.zeros_like(by_level)

    for s in range(mixed.shape[0]):
        grads = mixed[s, first:, :]
        features = normed[s, :rows, :]
        level = normed[s, rows:, :rows].astype(F32)
        level = level[:LINES] + level[LINES:]
        by_level[...] += dot(level.astype(BF16), grads, 1, 1)
        along = jnp.sum(
            grads.astype(F32) * projected[s, : 3 * first, :].astype(F32), axis=0, keepdims=True
        )
        drift = level * (along * (1.0 / width))
        drift = jnp.concatenate([drift, jnp.zeros_like(drift)], axis=0).astype(BF16)
        total[...] += dot(jnp.concatenate([grads, drift], axis=0), features, 1, 0)

    @pl.when(step == pl.num_programs(0) - 1)
    def _():
        tiles, _, part = out.shape
        for r in range(tiles):
            out[r] = (total[: 3 * first, r * part : (r + 1) * part] * factor).astype(BF16)
        scale = gain[...]
        drift = total[3 * first : 3 * first + LINES, :] / scale
        table = dot(by_level[...].astype(BF16), weight[0], 1, 0) * scale - drift
        table = table + local[...]
        for_gain = weight[0].astype(F32) * total[: 3 * first, :]
        for_gain = jnp.sum(for_gain, axis=0, keepdims=True) / scale
        line = lax.broadcasted_iota(jnp.int32, table.shape, 0)
        both = jnp.where(line == LINES - 1, for_gain, table) * factor
        for c in range(width // LANES):
            small[c * LINES : (c + 1) * LINES, :] = both[:, c * LANES : (c + 1) * LANES]


def weight_grad(head, mixed, projected, normed, weight, gain, local, tiles, factor):
    shards, four, rows = mixed.shape
    width = normed.shape[-1]
    first = four // 4
    lines = four - first
    each = 2
    shape = (tiles, lines, width // tiles)
    small = (width // LANES * LINES, LANES)

    def by_step(shape):
        return pl.BlockSpec((each,) + shape[1:], lambda i, h: (i, 0, 0))

    def fixed(shape):
        zeros = (0,) * len(shape)
        return pl.BlockSpec(shape, lambda i, h: zeros)

    return pl.pallas_call(
        functools.partial(weight_grad_body, factor=factor),
        grid_spec=pltpu.PrefetchScalarGridSpec(
            num_scalar_prefetch=1,
            grid=(shards // each,),
            in_specs=[by_step(part.shape) for part in (mixed, projected, normed)]
            + [
                pl.BlockSpec((1, lines, width), lambda i, h: (h[0], 0, 0)),
                fixed(gain.shape),
                fixed(local.shape),
            ],
            out_specs=[fixed(shape), fixed(small)],
            scratch_shapes=[
                pltpu.VMEM((lines + 2 * LINES, width), F32),
                pltpu.VMEM((LINES, lines), F32),
            ],
        ),
        out_shape=[
            jax.ShapeDtypeStruct(shape, BF16),
            jax.ShapeDtypeStruct(small, F32),
        ],
        compiler_params=vmem(60),
        name="weight_grad",
    )(head, mixed, projected, normed, weight, gain, local)


def out_grad_body(column, small, *refs, factor):
    out = refs[-1]
    ways = out.shape[0]
    attended, cotangents = refs[:ways], refs[ways : 2 * ways]
    shards, size, _ = attended[0].shape
    total = 0.0
    for k, cotangent in enumerate(cotangents):
        s = (column[0] + shards - k) % shards
        rows = jnp.concatenate([part[s] for part in attended], axis=0)
        total = total + dot(rows, cotangent[...], 1, 0)
    total = (total * factor).astype(BF16)
    tiles = total.shape[1] // LANES
    high = small[...].astype(BF16)
    low = (small[...] - high.astype(F32)).astype(BF16)
    for h in range(ways):
        for r in range(tiles):
            out[h, r * size : (r + 1) * size, :] = total[
                h * size : (h + 1) * size, r * LANES : (r + 1) * LANES
            ]
        out[h, tiles * size : tiles * size + high.shape[0], :] = high
        out[h, tiles * size + high.shape[0] :, :] = low


def out_grad(column, small, attended, cotangents, factor):
    _, size, _ = attended[0].shape
    tiles = cotangents[0].shape[-1] // LANES
    shape = (len(attended), tiles * size + 2 * small.shape[0], LANES)
    return pl.pallas_call(
        functools.partial(out_grad_body, factor=factor),
        in_specs=[pl.BlockSpec(memory_space=pltpu.SMEM)]
        + [pl.BlockSpec(memory_space=pltpu.VMEM)] * (1 + len(attended) + len(cotangents)),
        out_specs=pl.BlockSpec(memory_space=pltpu.VMEM),
        out_shape=jax.ShapeDtypeStruct(shape, BF16),
        compiler_params=vmem(48),
        name="out_grad",
    )(column, small, *attended, *cotangents)


def finish_output_body(mixed, weight, features, output, total):
    heads, size, rows = mixed.shape
    index = pl.program_id(0)

    @pl.when(index == 0)
    def _():
        total[...] = features[...].astype(F32)

    attended = mixed[...].reshape(heads * size, rows)
    total[...] += dot(attended, weight[...].reshape(heads * size, -1), 0, 0)

    @pl.when(index == pl.num_programs(0) - 1)
    def _():
        output[...] = total[...].astype(BF16)


def finish_output(mixed, weight, features):
    count, _, rows = mixed.shape
    _, size, width = weight.shape
    heads = 4
    return pl.pallas_call(
        finish_output_body,
        grid=(count // heads,),
        in_specs=[
            pl.BlockSpec((heads, size, rows), lambda i: (i, 0, 0)),
            pl.BlockSpec((heads, size, width), lambda i: (i, 0, 0)),
            whole((rows, width)),
        ],
        out_specs=whole((rows, width)),
        out_shape=jax.ShapeDtypeStruct((rows, width), BF16),
        scratch_shapes=[pltpu.VMEM((rows, width), F32)],
        compiler_params=vmem(60),
        name="finish_output",
    )(mixed, weight, features)


def finish_grad_body(mixed, weight, features, gain, cotangent, place, outgoing, total):
    heads, four, rows = mixed.shape
    size = four // 4
    index = pl.program_id(0)

    @pl.when(index == 0)
    def _():
        total[...] = jnp.zeros_like(total)

    grads = mixed[:, size:, :].reshape(heads * 3 * size, rows)
    total[...] += dot(grads, weight[...].reshape(heads * 3 * size, -1), 0, 0)

    @pl.when(index == pl.num_programs(0) - 1)
    def _():
        active = features[...].astype(F32)
        inverse = lax.rsqrt(jnp.mean(active * active, axis=1, keepdims=True) + EPSILON)
        scaled = gain[...] * total[...]
        cubed = inverse * inverse * inverse
        grad_active = inverse * scaled - active * cubed * jnp.mean(
            active * scaled, axis=1, keepdims=True
        )
        grad_features = (cotangent[...].astype(F32) + grad_active).astype(BF16)
        count = outgoing.shape[0] * outgoing.shape[1]
        slot = lax.broadcasted_iota(jnp.int32, (count, rows), 0)
        pick = jnp.where(slot == place[...], 1.0, 0.0).astype(BF16)
        outgoing[...] = dot(pick, grad_features, 1, 0).astype(BF16).reshape(outgoing.shape)


def finish_grad(mixed, weight, features, gain, cotangent, place, owners, slots):
    count, four, rows = mixed.shape
    width = features.shape[1]
    heads = 4
    return pl.pallas_call(
        finish_grad_body,
        grid=(count // heads,),
        in_specs=[
            pl.BlockSpec((heads, four, rows), lambda i: (i, 0, 0)),
            pl.BlockSpec((heads, four - four // 4, width), lambda i: (i, 0, 0)),
            whole((rows, width)),
            whole((1, width)),
            whole((rows, width)),
            whole((1, rows)),
        ],
        out_specs=whole((owners, slots, width)),
        out_shape=jax.ShapeDtypeStruct((owners, slots, width), BF16),
        scratch_shapes=[pltpu.VMEM((rows, width), F32)],
        compiler_params=vmem(60),
        name="finish_grad",
    )(mixed, weight, features, gain, cotangent, place)


def pick(value, k, axis=0):
    return lax.dynamic_index_in_dim(value, k, axis, keepdims=False)


def sum_to_tiles(value, small, tile_index):
    tiles, lines, lanes = value.shape
    ways = tiles // 2
    core, place = tile_index % 2, tile_index // 2
    value = value.reshape(ways, 2, lines, lanes)

    def mine(k):
        return pick(value, k, 1).reshape(ways * lines, lanes)

    other = jnp.concatenate([mine(1 - core), small], axis=0)
    other = lax.ppermute(other, "tile", [(i, i ^ 1) for i in range(tiles)])
    both = jnp.concatenate([mine(core), small], axis=0) + other
    value, small = both[: ways * lines].reshape(ways, lines, lanes), both[ways * lines :]
    parts = [jnp.concatenate([pick(value, place), small], axis=0)] + [
        lax.ppermute(
            jnp.concatenate([pick(value, (place + k) % ways), small], axis=0),
            "tile",
            [(i, (i + 2 * k) % tiles) for i in range(tiles)],
        )
        for k in range(1, ways)
    ]
    both = sum(parts[1:], parts[0])
    return both[:lines], both[lines:]


def on_device(
    tokens, levels, counts, level_table, norm_gain, project_weight, output_weight, cotangent
):
    tiles = lax.axis_size("tile")
    shards = lax.axis_size("seq")
    tile_index = lax.axis_index("tile")
    shard_index = lax.axis_index("seq")
    owners = tiles * shards
    slots = tokens.shape[3]
    width = tokens.shape[4]
    rows = cotangent.shape[1]
    length = rows * shards
    count, _, size, _ = project_weight.shape
    scale = 1.0 / math.sqrt(size)
    shift = math.log(length)
    factor = 1.0 / math.sqrt(tiles * length)
    kinds = level_table.shape[0]

    grad_rows = cotangent[0]
    side = math.isqrt(shards)
    line, column = shard_index // side, shard_index % side

    def along_line(value, k):
        return lax.ppermute(
            value, "seq", [(i, i // side * side + (i + k) % side) for i in range(shards)]
        )

    def along_column(value, k):
        return lax.ppermute(value, "seq", [(i, (i + k * side) % shards) for i in range(shards)])

    me = tile_index * shards + shard_index
    my_counts = lax.dynamic_index_in_dim(counts, me, 2, keepdims=False)
    used = jnp.arange(slots, dtype=jnp.int32) < my_counts[..., None]
    onehot = (levels[0][..., None] == jnp.arange(LANES, dtype=jnp.int32)).astype(BF16)
    embedded = tokens[0].astype(F32) + jnp.einsum(
        "msjl,ld->msjd", onehot[..., :kinds], level_table, preferred_element_type=F32
    )
    embedded = jnp.concatenate([embedded.astype(BF16), onehot], axis=-1)
    embedded = jnp.where(used[..., None], embedded, jnp.zeros((), BF16))
    received = lax.all_to_all(
        embedded.reshape(owners, slots, width + LANES),
        ("tile", "seq"),
        split_axis=0,
        concat_axis=0,
        tiled=True,
    )
    map_counts = lax.dynamic_index_in_dim(counts, tile_index, 0, keepdims=False)
    own_counts = lax.dynamic_index_in_dim(map_counts, shard_index, 0, keepdims=False)
    place = pack_positions(own_counts, rows, slots)
    gain = norm_gain.reshape(1, width)
    weight = project_weight.reshape(count, 3 * size, width)

    packed, features, normed, local = project(
        received,
        place.reshape(rows, 1),
        gain,
        grad_rows,
        weight,
        project_grads(grad_rows, output_weight),
    )
    by_head = lax.all_to_all(packed, "seq", split_axis=0, concat_axis=0, tiled=True)
    all_normed = lax.all_gather(normed, "seq")
    by_head, line_rows = lax.optimization_barrier((by_head, grad_rows))
    line_rows = [line_rows] + [along_line(line_rows, k) for k in range(1, side)]
    attended, head_attended = attend(by_head, scale, shift)
    attended, head_attended, line_rows = lax.optimization_barrier(
        (attended, head_attended, line_rows)
    )
    mixed = lax.all_to_all(attended, "seq", split_axis=0, concat_axis=0, tiled=True)

    shares, small = weight_grad(
        shard_index.reshape(1),
        attended,
        by_head,
        all_normed,
        weight,
        gain,
        local,
        tiles,
        factor,
    )
    head_attended = head_attended.reshape(side, side, size, rows)
    column_attended = [pick(head_attended, line)] + [
        along_column(pick(head_attended, (line + k) % side), k) for k in range(1, side)
    ]
    out_shares = out_grad(column.reshape(1), small, column_attended, line_rows, factor)
    out_shares = sum(
        [along_column(out_shares[k], -k).astype(F32) for k in range(1, side)],
        out_shares[0].astype(F32),
    )
    outgoing = finish_grad(
        mixed, weight, features, gain, grad_rows, place.reshape(1, rows), owners, slots
    )
    output = finish_output(mixed, output_weight, features)
    outgoing, out_shares, shares = lax.optimization_barrier((outgoing, out_shares, shares))
    returned = lax.all_to_all(
        outgoing,
        ("tile", "seq"),
        split_axis=0,
        concat_axis=0,
        tiled=True,
    )
    token_grad = returned.reshape(tiles, shards, slots, width)
    lines = tiles * size
    small_lines = (out_shares.shape[0] - lines) // 2
    small = out_shares[lines : lines + small_lines] + out_shares[lines + small_lines :]
    out_shares = out_shares[:lines].reshape(tiles, size, LANES)
    shares = jnp.concatenate([out_shares, shares.astype(F32)], axis=1)
    shares, small = sum_to_tiles(shares, small, tile_index)
    small = sum([along_line(small, k) for k in range(1, side)], small)
    small = small.reshape(width // LANES, LINES, LANES).transpose(1, 0, 2).reshape(LINES, width)
    return (
        output[None],
        token_grad[None],
        shares[size:].reshape(1, 3, size, width // tiles),
        shares[:size].reshape(1, size, width // tiles),
        small[LINES - 1],
        small[:kinds],
    )


def solution(mesh):
    return jax.shard_map(
        on_device,
        mesh=mesh,
        in_specs=(
            P(("tile", "seq"), None, None, None, None),
            P(("tile", "seq"), None, None, None),
            P(),
            P(),
            P(),
            P(),
            P(),
            P("tile", "seq", None),
        ),
        out_specs=(
            P("tile", "seq", None),
            P(("tile", "seq"), None, None, None, None),
            P("seq", None, None, "tile"),
            P("seq", None, "tile"),
            P(),
            P(),
        ),
        check_vma=False,
    )
```

```python
import functools
import math

import jax
import jax.numpy as jnp
from jax import lax
from jax.experimental import pallas as pl
from jax.experimental.pallas import tpu as pltpu
from jax.sharding import PartitionSpec as P

EPSILON = 1e-05
BF16 = jnp.bfloat16
F32 = jnp.float32
MIB = 2**20
LANES = 128
LINES = 8


def dot(a, b, ca, cb):
    return lax.dot_general(a, b, (((ca,), (cb,)), ((), ())), preferred_element_type=F32)


def whole(shape):
    zeros = (0,) * len(shape)
    return pl.BlockSpec(shape, lambda i: zeros)


def vmem(mib):
    return pltpu.CompilerParams(vmem_limit_bytes=mib * MIB)


def pack_positions(counts, rows, slots):
    starts = jnp.cumsum(counts) - counts
    place = jnp.arange(rows, dtype=jnp.int32)
    before = (starts[None, :] <= place[:, None]).astype(jnp.int32)
    owner = jnp.sum(before, axis=1) - 1
    first = jnp.max(jnp.where(before > 0, starts[None, :], 0), axis=1)
    return owner * slots + place - first


def project_body(
    received, place, gain, cotangent, weight, grads, packed, features, normed, local, heads
):
    rows, width = features.shape

    @pl.when(pl.program_id(0) == 0)
    def _():
        count = received.shape[0] * received.shape[1]
        slot = lax.broadcasted_iota(jnp.int32, (rows, count), 1)
        pick = jnp.where(slot == place[...], 1.0, 0.0).astype(BF16)
        taken = dot(pick, received[...].reshape(count, received.shape[2]), 1, 0)
        active = taken[:, :width]
        features[...] = active.astype(BF16)
        level = taken[:, width:]
        inverse = lax.rsqrt(jnp.mean(active * active, axis=1, keepdims=True) + EPSILON)
        normed[:rows, :] = (active * inverse * gain[...]).astype(BF16)
        kept = jnp.transpose(level * inverse)[:LINES]
        kept = jnp.concatenate([kept, kept - kept.astype(BF16).astype(F32)], axis=0)
        normed[rows:, :rows] = kept.astype(BF16)
        normed[rows:, rows:] = jnp.zeros((2 * LINES, width - rows), BF16)
        local[...] = dot(level.astype(BF16), cotangent[...], 0, 0)[:LINES]

    size = grads.shape[1]
    rows, width = features.shape
    projected = dot(weight[...].reshape(heads * 3 * size, width), normed[:rows, :], 1, 1)
    packed[:, : 3 * size, :] = projected.astype(BF16).reshape(heads, 3 * size, rows)
    packed[:, 3 * size :, :] = grads[...]


def project_grads_body(cotangent, weight, out):
    heads, size, rows = out.shape
    grads = dot(weight[...].reshape(heads * size, -1), cotangent[...], 1, 1)
    out[...] = grads.astype(BF16).reshape(heads, size, rows)


def project_grads(cotangent, weight):
    rows, width = cotangent.shape
    count, size, _ = weight.shape
    heads = 4
    return pl.pallas_call(
        project_grads_body,
        grid=(count // heads,),
        in_specs=[
            whole((rows, width)),
            pl.BlockSpec((heads, size, width), lambda i: (i, 0, 0)),
        ],
        out_specs=pl.BlockSpec((heads, size, rows), lambda i: (i, 0, 0)),
        out_shape=jax.ShapeDtypeStruct((count, size, rows), BF16),
        compiler_params=vmem(60),
        name="project_grads",
    )(cotangent, weight)


def project(received, place, gain, cotangent, weight, grads):
    rows, width = cotangent.shape
    count, three, _ = weight.shape
    size = grads.shape[1]
    heads = 4
    return pl.pallas_call(
        functools.partial(project_body, heads=heads),
        grid=(count // heads,),
        in_specs=[
            whole(received.shape),
            whole((rows, 1)),
            whole((1, width)),
            whole((rows, width)),
            pl.BlockSpec((heads, three, width), lambda i: (i, 0, 0)),
            pl.BlockSpec((heads, size, rows), lambda i: (i, 0, 0)),
        ],
        out_specs=[
            pl.BlockSpec((heads, three + size, rows), lambda i: (i, 0, 0)),
            whole((rows, width)),
            whole((rows + 2 * LINES, width)),
            whole((LINES, width)),
        ],
        out_shape=[
            jax.ShapeDtypeStruct((count, three + size, rows), BF16),
            jax.ShapeDtypeStruct((rows, width), BF16),
            jax.ShapeDtypeStruct((rows + 2 * LINES, width), BF16),
            jax.ShapeDtypeStruct((LINES, width), F32),
        ],
        compiler_params=vmem(60),
        name="project",
    )(received, place, gain, cotangent, weight, grads)


def attend_body(
    source,
    out,
    only,
    packed,
    query,
    grad,
    keys,
    values,
    key_total,
    value_total,
    arrived,
    *,
    scale,
    shift,
    step,
):
    shards, four, rows = packed.shape
    copies = [
        pltpu.make_async_copy(source.at[s], packed.at[s], arrived.at[s]) for s in range(shards)
    ]
    for copy in copies:
        copy.start()
    size = four // 4
    length = shards * rows
    rate = scale * math.log2(math.e)
    offset = shift * math.log2(math.e)
    key_total[...] = jnp.zeros_like(key_total)
    value_total[...] = jnp.zeros_like(value_total)
    for s in range(shards):
        copies[s].wait()
        part = slice(s * rows, (s + 1) * rows)
        query[part, :] = jnp.transpose(packed[s, :size, :])
        grad[part, :] = jnp.transpose(packed[s, 3 * size :, :])
        keys[:, part] = packed[s, size : 2 * size, :]
        values[:, part] = packed[s, 2 * size : 3 * size, :]

    def one_block(i, _):
        mine = pl.ds(pl.multiple_of(i * rows, rows), rows)
        q, g = query[mine, :], grad[mine, :]
        q_across, g_across = packed[i, :size, :], packed[i, 3 * size :, :]

        attended = jnp.zeros((size, rows), F32)
        grad_query = jnp.zeros((size, rows), F32)
        for j in range(length // step):
            part = slice(j * step, (j + 1) * step)
            k, v = keys[:, part], values[:, part]
            odds = jnp.exp2(offset - dot(q, k, 1, 0) * rate)
            probs = pl.reciprocal(1.0 + odds, approx=True)
            weights = probs.astype(BF16)
            slope = probs - probs * probs
            grad_scores = (dot(g, v, 1, 0) * slope).astype(BF16)
            attended = attended + dot(v, weights, 1, 1)
            grad_query = grad_query + dot(k, grad_scores, 1, 1)
            key_total[:, part] += dot(q_across, grad_scores, 1, 0)
            value_total[:, part] += dot(g_across, weights, 1, 0)
        out[i, :size, :] = attended.astype(BF16)
        only[i] = attended.astype(BF16)
        out[i, size : 2 * size, :] = (grad_query * scale).astype(BF16)
        return 0

    lax.fori_loop(0, shards, one_block, 0)
    for s in range(shards):
        part = slice(s * rows, (s + 1) * rows)
        out[s, 2 * size : 3 * size, :] = (key_total[:, part] * scale).astype(BF16)
        out[s, 3 * size :, :] = value_total[:, part].astype(BF16)


def attend(packed, scale, shift):
    shards, four, rows = packed.shape
    size, length = four // 4, shards * rows
    return pl.pallas_call(
        functools.partial(attend_body, scale=scale, shift=shift, step=min(1024, length)),
        in_specs=[pl.BlockSpec(memory_space=pl.ANY)],
        out_specs=[pl.BlockSpec(memory_space=pltpu.VMEM)] * 2,
        out_shape=[
            jax.ShapeDtypeStruct(packed.shape, BF16),
            jax.ShapeDtypeStruct((shards, size, rows), BF16),
        ],
        scratch_shapes=[
            pltpu.VMEM(packed.shape, BF16),
            pltpu.VMEM((length, size), BF16),
            pltpu.VMEM((length, size), BF16),
            pltpu.VMEM((size, length), BF16),
            pltpu.VMEM((size, length), BF16),
            pltpu.VMEM((size, length), F32),
            pltpu.VMEM((size, length), F32),
            pltpu.SemaphoreType.DMA((shards,)),
        ],
        compiler_params=vmem(60),
        cost_estimate=pl.CostEstimate(
            flops=48 * length * length * size, bytes_accessed=8 * length * size, transcendentals=0
        ),
        name="attend",
    )(packed)


def weight_grad_body(
    head,
    mixed,
    projected,
    normed,
    weight,
    gain,
    local,
    out,
    small,
    total,
    by_level,
    *,
    factor,
):
    del head
    step = pl.program_id(0)
    rows = mixed.shape[2]
    first = mixed.shape[1] // 4
    width = normed.shape[2]

    @pl.when(step == 0)
    def _():
        total[...] = jnp.zeros_like(total)
        by_level[...] = jnp.zeros_like(by_level)

    for s in range(mixed.shape[0]):
        grads = mixed[s, first:, :]
        features = normed[s, :rows, :]
        level = normed[s, rows:, :rows].astype(F32)
        level = level[:LINES] + level[LINES:]
        by_level[...] += dot(level.astype(BF16), grads, 1, 1)
        along = jnp.sum(
            grads.astype(F32) * projected[s, : 3 * first, :].astype(F32), axis=0, keepdims=True
        )
        drift = level * (along * (1.0 / width))
        drift = jnp.concatenate([drift, jnp.zeros_like(drift)], axis=0).astype(BF16)
        total[...] += dot(jnp.concatenate([grads, drift], axis=0), features, 1, 0)

    @pl.when(step == pl.num_programs(0) - 1)
    def _():
        tiles, _, part = out.shape
        for r in range(tiles):
            out[r] = (total[: 3 * first, r * part : (r + 1) * part] * factor).astype(BF16)
        scale = gain[...]
        drift = total[3 * first : 3 * first + LINES, :] / scale
        table = dot(by_level[...].astype(BF16), weight[0], 1, 0) * scale - drift
        table = table + local[...]
        for_gain = weight[0].astype(F32) * total[: 3 * first, :]
        for_gain = jnp.sum(for_gain, axis=0, keepdims=True) / scale
        line = lax.broadcasted_iota(jnp.int32, table.shape, 0)
        both = jnp.where(line == LINES - 1, for_gain, table) * factor
        for c in range(width // LANES):
            small[c * LINES : (c + 1) * LINES, :] = both[:, c * LANES : (c + 1) * LANES]


def weight_grad(head, mixed, projected, normed, weight, gain, local, tiles, factor):
    shards, four, rows = mixed.shape
    width = normed.shape[-1]
    first = four // 4
    lines = four - first
    each = 2
    shape = (tiles, lines, width // tiles)
    small = (width // LANES * LINES, LANES)

    def by_step(shape):
        return pl.BlockSpec((each,) + shape[1:], lambda i, h: (i, 0, 0))

    def fixed(shape):
        zeros = (0,) * len(shape)
        return pl.BlockSpec(shape, lambda i, h: zeros)

    return pl.pallas_call(
        functools.partial(weight_grad_body, factor=factor),
        grid_spec=pltpu.PrefetchScalarGridSpec(
            num_scalar_prefetch=1,
            grid=(shards // each,),
            in_specs=[by_step(part.shape) for part in (mixed, projected, normed)]
            + [
                pl.BlockSpec((1, lines, width), lambda i, h: (h[0], 0, 0)),
                fixed(gain.shape),
                fixed(local.shape),
            ],
            out_specs=[fixed(shape), fixed(small)],
            scratch_shapes=[
                pltpu.VMEM((lines + 2 * LINES, width), F32),
                pltpu.VMEM((LINES, lines), F32),
            ],
        ),
        out_shape=[
            jax.ShapeDtypeStruct(shape, BF16),
            jax.ShapeDtypeStruct(small, F32),
        ],
        compiler_params=vmem(60),
        name="weight_grad",
    )(head, mixed, projected, normed, weight, gain, local)


def out_grad_body(column, small, *refs, factor):
    out = refs[-1]
    ways = out.shape[0]
    attended, cotangents = refs[:ways], refs[ways : 2 * ways]
    shards, size, _ = attended[0].shape
    total = 0.0
    for k, cotangent in enumerate(cotangents):
        s = (column[0] + shards - k) % shards
        rows = jnp.concatenate([part[s] for part in attended], axis=0)
        total = total + dot(rows, cotangent[...], 1, 0)
    total = (total * factor).astype(BF16)
    tiles = total.shape[1] // LANES
    high = small[...].astype(BF16)
    low = (small[...] - high.astype(F32)).astype(BF16)
    for h in range(ways):
        for r in range(tiles):
            out[h, r * size : (r + 1) * size, :] = total[
                h * size : (h + 1) * size, r * LANES : (r + 1) * LANES
            ]
        out[h, tiles * size : tiles * size + high.shape[0], :] = high
        out[h, tiles * size + high.shape[0] :, :] = low


def out_grad(column, small, attended, cotangents, factor):
    _, size, _ = attended[0].shape
    tiles = cotangents[0].shape[-1] // LANES
    shape = (len(attended), tiles * size + 2 * small.shape[0], LANES)
    return pl.pallas_call(
        functools.partial(out_grad_body, factor=factor),
        in_specs=[pl.BlockSpec(memory_space=pltpu.SMEM)]
        + [pl.BlockSpec(memory_space=pltpu.VMEM)] * (1 + len(attended) + len(cotangents)),
        out_specs=pl.BlockSpec(memory_space=pltpu.VMEM),
        out_shape=jax.ShapeDtypeStruct(shape, BF16),
        compiler_params=vmem(48),
        name="out_grad",
    )(column, small, *attended, *cotangents)


def finish_output_body(mixed, weight, features, output, total):
    heads, size, rows = mixed.shape
    index = pl.program_id(0)

    @pl.when(index == 0)
    def _():
        total[...] = features[...].astype(F32)

    attended = mixed[...].reshape(heads * size, rows)
    total[...] += dot(attended, weight[...].reshape(heads * size, -1), 0, 0)

    @pl.when(index == pl.num_programs(0) - 1)
    def _():
        output[...] = total[...].astype(BF16)


def finish_output(mixed, weight, features):
    count, _, rows = mixed.shape
    _, size, width = weight.shape
    heads = 4
    return pl.pallas_call(
        finish_output_body,
        grid=(count // heads,),
        in_specs=[
            pl.BlockSpec((heads, size, rows), lambda i: (i, 0, 0)),
            pl.BlockSpec((heads, size, width), lambda i: (i, 0, 0)),
            whole((rows, width)),
        ],
        out_specs=whole((rows, width)),
        out_shape=jax.ShapeDtypeStruct((rows, width), BF16),
        scratch_shapes=[pltpu.VMEM((rows, width), F32)],
        compiler_params=vmem(60),
        cost_estimate=pl.CostEstimate(flops=1, bytes_accessed=1, transcendentals=0),
        name="finish_output",
    )(mixed, weight, features)


def finish_grad_body(mixed, weight, features, gain, cotangent, place, outgoing, total):
    heads, four, rows = mixed.shape
    size = four // 4
    index = pl.program_id(0)

    @pl.when(index == 0)
    def _():
        total[...] = jnp.zeros_like(total)

    grads = mixed[:, size:, :].reshape(heads * 3 * size, rows)
    total[...] += dot(grads, weight[...].reshape(heads * 3 * size, -1), 0, 0)

    @pl.when(index == pl.num_programs(0) - 1)
    def _():
        active = features[...].astype(F32)
        inverse = lax.rsqrt(jnp.mean(active * active, axis=1, keepdims=True) + EPSILON)
        scaled = gain[...] * total[...]
        cubed = inverse * inverse * inverse
        grad_active = inverse * scaled - active * cubed * jnp.mean(
            active * scaled, axis=1, keepdims=True
        )
        grad_features = (cotangent[...].astype(F32) + grad_active).astype(BF16)
        count = outgoing.shape[0] * outgoing.shape[1]
        slot = lax.broadcasted_iota(jnp.int32, (count, rows), 0)
        pick = jnp.where(slot == place[...], 1.0, 0.0).astype(BF16)
        outgoing[...] = dot(pick, grad_features, 1, 0).astype(BF16).reshape(outgoing.shape)


def finish_grad(mixed, weight, features, gain, cotangent, place, owners, slots):
    count, four, rows = mixed.shape
    width = features.shape[1]
    heads = 4
    return pl.pallas_call(
        finish_grad_body,
        grid=(count // heads,),
        in_specs=[
            pl.BlockSpec((heads, four, rows), lambda i: (i, 0, 0)),
            pl.BlockSpec((heads, four - four // 4, width), lambda i: (i, 0, 0)),
            whole((rows, width)),
            whole((1, width)),
            whole((rows, width)),
            whole((1, rows)),
        ],
        out_specs=whole((owners, slots, width)),
        out_shape=jax.ShapeDtypeStruct((owners, slots, width), BF16),
        scratch_shapes=[pltpu.VMEM((rows, width), F32)],
        compiler_params=vmem(60),
        name="finish_grad",
    )(mixed, weight, features, gain, cotangent, place)


def pick(value, k, axis=0):
    return lax.dynamic_index_in_dim(value, k, axis, keepdims=False)


def sum_to_tiles(value, small, tile_index):
    tiles, lines, lanes = value.shape
    ways = tiles // 2
    core, place = tile_index % 2, tile_index // 2
    value = value.reshape(ways, 2, lines, lanes)

    def mine(k):
        return pick(value, k, 1).reshape(ways * lines, lanes)

    other = jnp.concatenate([mine(1 - core), small], axis=0)
    other = lax.ppermute(other, "tile", [(i, i ^ 1) for i in range(tiles)])
    both = jnp.concatenate([mine(core), small], axis=0) + other
    value, small = both[: ways * lines].reshape(ways, lines, lanes), both[ways * lines :]
    parts = [jnp.concatenate([pick(value, place), small], axis=0)] + [
        lax.ppermute(
            jnp.concatenate([pick(value, (place + k) % ways), small], axis=0),
            "tile",
            [(i, (i + 2 * k) % tiles) for i in range(tiles)],
        )
        for k in range(1, ways)
    ]
    both = sum(parts[1:], parts[0])
    return both[:lines], both[lines:]


def on_device(
    tokens, levels, counts, level_table, norm_gain, project_weight, output_weight, cotangent
):
    tiles = lax.axis_size("tile")
    shards = lax.axis_size("seq")
    tile_index = lax.axis_index("tile")
    shard_index = lax.axis_index("seq")
    owners = tiles * shards
    slots = tokens.shape[3]
    width = tokens.shape[4]
    rows = cotangent.shape[1]
    length = rows * shards
    count, _, size, _ = project_weight.shape
    scale = 1.0 / math.sqrt(size)
    shift = math.log(length)
    factor = 1.0 / math.sqrt(tiles * length)
    kinds = level_table.shape[0]

    grad_rows = cotangent[0]
    side = math.isqrt(shards)
    line, column = shard_index // side, shard_index % side

    def along_line(value, k):
        return lax.ppermute(
            value, "seq", [(i, i // side * side + (i + k) % side) for i in range(shards)]
        )

    def along_column(value, k):
        return lax.ppermute(value, "seq", [(i, (i + k * side) % shards) for i in range(shards)])

    onehot = (levels[0][..., None] == jnp.arange(LANES, dtype=jnp.int32)).astype(BF16)
    embedded = tokens[0].astype(F32) + jnp.einsum(
        "msjl,ld->msjd", onehot[..., :kinds], level_table, preferred_element_type=F32
    )
    embedded = jnp.concatenate([embedded.astype(BF16), onehot], axis=-1)
    received = lax.all_to_all(
        embedded.reshape(owners, slots, width + LANES),
        ("tile", "seq"),
        split_axis=0,
        concat_axis=0,
        tiled=True,
    )
    map_counts = lax.dynamic_index_in_dim(counts, tile_index, 0, keepdims=False)
    own_counts = lax.dynamic_index_in_dim(map_counts, shard_index, 0, keepdims=False)
    place = pack_positions(own_counts, rows, slots)
    gain = norm_gain.reshape(1, width)
    weight = project_weight.reshape(count, 3 * size, width)

    packed, features, normed, local = project(
        received,
        place.reshape(rows, 1),
        gain,
        grad_rows,
        weight,
        project_grads(grad_rows, output_weight),
    )
    by_head = lax.all_to_all(packed, "seq", split_axis=0, concat_axis=0, tiled=True)
    all_normed = lax.all_gather(normed, "seq")
    by_head, line_rows = lax.optimization_barrier((by_head, grad_rows))
    line_rows = [line_rows] + [along_line(line_rows, k) for k in range(1, side)]
    attended, head_attended = attend(by_head, scale, shift)
    attended, head_attended, line_rows = lax.optimization_barrier(
        (attended, head_attended, line_rows)
    )
    mixed = lax.all_to_all(attended, "seq", split_axis=0, concat_axis=0, tiled=True)

    shares, small = weight_grad(
        shard_index.reshape(1),
        attended,
        by_head,
        all_normed,
        weight,
        gain,
        local,
        tiles,
        factor,
    )
    head_attended = head_attended.reshape(side, side, size, rows)
    column_attended = [pick(head_attended, line)] + [
        along_column(pick(head_attended, (line + k) % side), k) for k in range(1, side)
    ]
    out_shares = out_grad(column.reshape(1), small, column_attended, line_rows, factor)
    out_shares = sum(
        [along_column(out_shares[k], -k).astype(F32) for k in range(1, side)],
        out_shares[0].astype(F32),
    )
    outgoing = finish_grad(
        mixed, weight, features, gain, grad_rows, place.reshape(1, rows), owners, slots
    )
    output = finish_output(mixed, output_weight, features)
    outgoing, out_shares, shares = lax.optimization_barrier((outgoing, out_shares, shares))
    returned = lax.all_to_all(
        outgoing,
        ("tile", "seq"),
        split_axis=0,
        concat_axis=0,
        tiled=True,
    )
    token_grad = returned.reshape(tiles, shards, slots, width)
    lines = tiles * size
    small_lines = (out_shares.shape[0] - lines) // 2
    small = out_shares[lines : lines + small_lines] + out_shares[lines + small_lines :]
    out_shares = out_shares[:lines].reshape(tiles, size, LANES)
    shares = jnp.concatenate([out_shares, shares.astype(F32)], axis=1)
    shares, small = sum_to_tiles(shares, small, tile_index)
    small = sum([along_line(small, k) for k in range(1, side)], small)
    small = small.reshape(width // LANES, LINES, LANES).transpose(1, 0, 2).reshape(LINES, width)
    return (
        output[None],
        token_grad[None],
        shares[size:].reshape(1, 3, size, width // tiles),
        shares[:size].reshape(1, size, width // tiles),
        small[LINES - 1],
        small[:kinds],
    )


def solution(mesh):
    return jax.shard_map(
        on_device,
        mesh=mesh,
        in_specs=(
            P(("tile", "seq"), None, None, None, None),
            P(("tile", "seq"), None, None, None),
            P(),
            P(),
            P(),
            P(),
            P(),
            P("tile", "seq", None),
        ),
        out_specs=(
            P("tile", "seq", None),
            P(("tile", "seq"), None, None, None, None),
            P("seq", None, None, "tile"),
            P("seq", None, "tile"),
            P(),
            P(),
        ),
        check_vma=False,
    )
```

```python
import functools
import math

import jax
import jax.numpy as jnp
from jax import lax
from jax.experimental import pallas as pl
from jax.experimental.pallas import tpu as pltpu
from jax.sharding import PartitionSpec as P

EPSILON = 1e-05
BF16 = jnp.bfloat16
F32 = jnp.float32
MIB = 2**20
LANES = 128
LINES = 8


def dot(a, b, ca, cb):
    return lax.dot_general(a, b, (((ca,), (cb,)), ((), ())), preferred_element_type=F32)


def whole(shape):
    zeros = (0,) * len(shape)
    return pl.BlockSpec(shape, lambda i: zeros)


def vmem(mib):
    return pltpu.CompilerParams(vmem_limit_bytes=mib * MIB)


def pack_positions(counts, rows, slots):
    starts = jnp.cumsum(counts) - counts
    place = jnp.arange(rows, dtype=jnp.int32)
    before = (starts[None, :] <= place[:, None]).astype(jnp.int32)
    owner = jnp.sum(before, axis=1) - 1
    first = jnp.max(jnp.where(before > 0, starts[None, :], 0), axis=1)
    return owner * slots + place - first


def project_body(
    received, place, gain, cotangent, weight, grads, packed, features, normed, local, heads
):
    rows, width = features.shape

    @pl.when(pl.program_id(0) == 0)
    def _():
        count = received.shape[0] * received.shape[1]
        slot = lax.broadcasted_iota(jnp.int32, (rows, count), 1)
        pick = jnp.where(slot == place[...], 1.0, 0.0).astype(BF16)
        taken = dot(pick, received[...].reshape(count, received.shape[2]), 1, 0)
        active = taken[:, :width]
        features[...] = active.astype(BF16)
        level = taken[:, width:]
        inverse = lax.rsqrt(jnp.mean(active * active, axis=1, keepdims=True) + EPSILON)
        normed[:rows, :] = (active * inverse * gain[...]).astype(BF16)
        kept = jnp.transpose(level * inverse)[:LINES]
        kept = jnp.concatenate([kept, kept - kept.astype(BF16).astype(F32)], axis=0)
        normed[rows:, :rows] = kept.astype(BF16)
        normed[rows:, rows:] = jnp.zeros((2 * LINES, width - rows), BF16)
        local[...] = dot(level.astype(BF16), cotangent[...], 0, 0)[:LINES]

    size = grads.shape[1]
    rows, width = features.shape
    projected = dot(weight[...].reshape(heads * 3 * size, width), normed[:rows, :], 1, 1)
    packed[:, : 3 * size, :] = projected.astype(BF16).reshape(heads, 3 * size, rows)
    packed[:, 3 * size :, :] = grads[...]


def project_grads_body(cotangent, weight, out):
    heads, size, rows = out.shape
    grads = dot(weight[...].reshape(heads * size, -1), cotangent[...], 1, 1)
    out[...] = grads.astype(BF16).reshape(heads, size, rows)


def project_grads(cotangent, weight):
    rows, width = cotangent.shape
    count, size, _ = weight.shape
    heads = 4
    return pl.pallas_call(
        project_grads_body,
        grid=(count // heads,),
        in_specs=[
            whole((rows, width)),
            pl.BlockSpec((heads, size, width), lambda i: (i, 0, 0)),
        ],
        out_specs=pl.BlockSpec((heads, size, rows), lambda i: (i, 0, 0)),
        out_shape=jax.ShapeDtypeStruct((count, size, rows), BF16),
        compiler_params=vmem(60),
        name="project_grads",
    )(cotangent, weight)


def project(received, place, gain, cotangent, weight, grads):
    rows, width = cotangent.shape
    count, three, _ = weight.shape
    size = grads.shape[1]
    heads = 4
    return pl.pallas_call(
        functools.partial(project_body, heads=heads),
        grid=(count // heads,),
        in_specs=[
            whole(received.shape),
            whole((rows, 1)),
            whole((1, width)),
            whole((rows, width)),
            pl.BlockSpec((heads, three, width), lambda i: (i, 0, 0)),
            pl.BlockSpec((heads, size, rows), lambda i: (i, 0, 0)),
        ],
        out_specs=[
            pl.BlockSpec((heads, three + size, rows), lambda i: (i, 0, 0)),
            whole((rows, width)),
            whole((rows + 2 * LINES, width)),
            whole((LINES, width)),
        ],
        out_shape=[
            jax.ShapeDtypeStruct((count, three + size, rows), BF16),
            jax.ShapeDtypeStruct((rows, width), BF16),
            jax.ShapeDtypeStruct((rows + 2 * LINES, width), BF16),
            jax.ShapeDtypeStruct((LINES, width), F32),
        ],
        compiler_params=vmem(60),
        name="project",
    )(received, place, gain, cotangent, weight, grads)


def attend_body(
    source,
    out,
    packed,
    by_query,
    by_key,
    query,
    grad,
    keys,
    values,
    key_total,
    value_total,
    arrived,
    left,
    *,
    scale,
    shift,
    step,
):
    shards, four, rows = packed.shape
    copies = [
        pltpu.make_async_copy(source.at[s], packed.at[s], arrived.at[s]) for s in range(shards)
    ]
    for copy in copies:
        copy.start()

    def leave(s):
        rows = pl.ds(0, by_query.shape[1])
        return pltpu.make_async_copy(by_query.at[s], out.at[s, rows], left.at[0, s])

    def leave_last(s):
        rows = pl.ds(by_query.shape[1], by_key.shape[1])
        return pltpu.make_async_copy(by_key.at[s], out.at[s, rows], left.at[1, s])

    size = four // 4
    length = shards * rows
    rate = scale * math.log2(math.e)
    offset = shift * math.log2(math.e)
    key_total[...] = jnp.zeros_like(key_total)
    value_total[...] = jnp.zeros_like(value_total)
    for s in range(shards):
        copies[s].wait()
        part = slice(s * rows, (s + 1) * rows)
        query[part, :] = jnp.transpose(packed[s, :size, :])
        grad[part, :] = jnp.transpose(packed[s, 3 * size :, :])
        keys[:, part] = packed[s, size : 2 * size, :]
        values[:, part] = packed[s, 2 * size : 3 * size, :]

    def one_block(i, _):
        mine = pl.ds(pl.multiple_of(i * rows, rows), rows)
        q, g = query[mine, :], grad[mine, :]
        q_across, g_across = packed[i, :size, :], packed[i, 3 * size :, :]

        attended = jnp.zeros((size, rows), F32)
        grad_query = jnp.zeros((size, rows), F32)
        for j in range(length // step):
            part = slice(j * step, (j + 1) * step)
            k, v = keys[:, part], values[:, part]
            odds = jnp.exp2(offset - dot(q, k, 1, 0) * rate)
            probs = pl.reciprocal(1.0 + odds, approx=True)
            weights = probs.astype(BF16)
            slope = probs - probs * probs
            grad_scores = (dot(g, v, 1, 0) * slope).astype(BF16)
            attended = attended + dot(v, weights, 1, 1)
            grad_query = grad_query + dot(k, grad_scores, 1, 1)
            key_total[:, part] += dot(q_across, grad_scores, 1, 0)
            value_total[:, part] += dot(g_across, weights, 1, 0)
        by_query[i, :size, :] = attended.astype(BF16)
        by_query[i, size:, :] = (grad_query * scale).astype(BF16)
        leave(i).start()
        return 0

    lax.fori_loop(0, shards, one_block, 0)
    for s in range(shards):
        part = slice(s * rows, (s + 1) * rows)
        by_key[s, :size, :] = (key_total[:, part] * scale).astype(BF16)
        by_key[s, size:, :] = value_total[:, part].astype(BF16)
        leave_last(s).start()
    for s in range(shards):
        leave(s).wait()
        leave_last(s).wait()


def attend(packed, scale, shift):
    shards, four, rows = packed.shape
    size, length = four // 4, shards * rows
    return pl.pallas_call(
        functools.partial(attend_body, scale=scale, shift=shift, step=min(1024, length)),
        in_specs=[pl.BlockSpec(memory_space=pl.ANY)],
        out_specs=pl.BlockSpec(memory_space=pl.ANY),
        out_shape=jax.ShapeDtypeStruct(packed.shape, BF16),
        scratch_shapes=[
            pltpu.VMEM(packed.shape, BF16),
            pltpu.VMEM((shards, 2 * size, rows), BF16),
            pltpu.VMEM((shards, 2 * size, rows), BF16),
            pltpu.VMEM((length, size), BF16),
            pltpu.VMEM((length, size), BF16),
            pltpu.VMEM((size, length), BF16),
            pltpu.VMEM((size, length), BF16),
            pltpu.VMEM((size, length), F32),
            pltpu.VMEM((size, length), F32),
            pltpu.SemaphoreType.DMA((shards,)),
            pltpu.SemaphoreType.DMA((2, shards)),
        ],
        compiler_params=vmem(60),
        cost_estimate=pl.CostEstimate(
            flops=48 * length * length * size, bytes_accessed=8 * length * size, transcendentals=0
        ),
        name="attend",
    )(packed)


def weight_grad_body(
    head,
    mixed,
    projected,
    normed,
    weight,
    gain,
    local,
    out,
    small,
    total,
    by_level,
    *,
    factor,
):
    del head
    step = pl.program_id(0)
    rows = mixed.shape[2]
    first = mixed.shape[1] // 4
    width = normed.shape[2]

    @pl.when(step == 0)
    def _():
        total[...] = jnp.zeros_like(total)
        by_level[...] = jnp.zeros_like(by_level)

    for s in range(mixed.shape[0]):
        grads = mixed[s, first:, :]
        features = normed[s, :rows, :]
        level = normed[s, rows:, :rows].astype(F32)
        level = level[:LINES] + level[LINES:]
        by_level[...] += dot(level.astype(BF16), grads, 1, 1)
        along = jnp.sum(
            grads.astype(F32) * projected[s, : 3 * first, :].astype(F32), axis=0, keepdims=True
        )
        drift = level * (along * (1.0 / width))
        drift = jnp.concatenate([drift, jnp.zeros_like(drift)], axis=0).astype(BF16)
        total[...] += dot(jnp.concatenate([grads, drift], axis=0), features, 1, 0)

    @pl.when(step == pl.num_programs(0) - 1)
    def _():
        tiles, _, part = out.shape
        for r in range(tiles):
            out[r] = (total[: 3 * first, r * part : (r + 1) * part] * factor).astype(BF16)
        scale = gain[...]
        drift = total[3 * first : 3 * first + LINES, :] / scale
        table = dot(by_level[...].astype(BF16), weight[0], 1, 0) * scale - drift
        table = table + local[...]
        for_gain = weight[0].astype(F32) * total[: 3 * first, :]
        for_gain = jnp.sum(for_gain, axis=0, keepdims=True) / scale
        line = lax.broadcasted_iota(jnp.int32, table.shape, 0)
        both = jnp.where(line == LINES - 1, for_gain, table) * factor
        for c in range(width // LANES):
            small[c * LINES : (c + 1) * LINES, :] = both[:, c * LANES : (c + 1) * LANES]


def weight_grad(head, mixed, projected, normed, weight, gain, local, tiles, factor):
    shards, four, rows = mixed.shape
    width = normed.shape[-1]
    first = four // 4
    lines = four - first
    each = 2
    shape = (tiles, lines, width // tiles)
    small = (width // LANES * LINES, LANES)

    def by_step(shape):
        return pl.BlockSpec((each,) + shape[1:], lambda i, h: (i, 0, 0))

    def fixed(shape):
        zeros = (0,) * len(shape)
        return pl.BlockSpec(shape, lambda i, h: zeros)

    return pl.pallas_call(
        functools.partial(weight_grad_body, factor=factor),
        grid_spec=pltpu.PrefetchScalarGridSpec(
            num_scalar_prefetch=1,
            grid=(shards // each,),
            in_specs=[by_step(part.shape) for part in (mixed, projected, normed)]
            + [
                pl.BlockSpec((1, lines, width), lambda i, h: (h[0], 0, 0)),
                fixed(gain.shape),
                fixed(local.shape),
            ],
            out_specs=[fixed(shape), fixed(small)],
            scratch_shapes=[
                pltpu.VMEM((lines + 2 * LINES, width), F32),
                pltpu.VMEM((LINES, lines), F32),
            ],
        ),
        out_shape=[
            jax.ShapeDtypeStruct(shape, BF16),
            jax.ShapeDtypeStruct(small, F32),
        ],
        compiler_params=vmem(60),
        name="weight_grad",
    )(head, mixed, projected, normed, weight, gain, local)


def out_grad_body(column, small, *refs, factor):
    out = refs[-1]
    ways = out.shape[0]
    attended, cotangents = refs[:ways], refs[ways : 2 * ways]
    shards, size, _ = attended[0].shape
    total = 0.0
    for k, cotangent in enumerate(cotangents):
        s = (column[0] + shards - k) % shards
        rows = jnp.concatenate([part[s] for part in attended], axis=0)
        total = total + dot(rows, cotangent[...], 1, 0)
    total = (total * factor).astype(BF16)
    tiles = total.shape[1] // LANES
    high = small[...].astype(BF16)
    low = (small[...] - high.astype(F32)).astype(BF16)
    for h in range(ways):
        for r in range(tiles):
            out[h, r * size : (r + 1) * size, :] = total[
                h * size : (h + 1) * size, r * LANES : (r + 1) * LANES
            ]
        out[h, tiles * size : tiles * size + high.shape[0], :] = high
        out[h, tiles * size + high.shape[0] :, :] = low


def out_grad(column, small, attended, cotangents, factor):
    _, size, _ = attended[0].shape
    tiles = cotangents[0].shape[-1] // LANES
    shape = (len(attended), tiles * size + 2 * small.shape[0], LANES)
    return pl.pallas_call(
        functools.partial(out_grad_body, factor=factor),
        in_specs=[pl.BlockSpec(memory_space=pltpu.SMEM)]
        + [pl.BlockSpec(memory_space=pltpu.VMEM)] * (1 + len(attended) + len(cotangents)),
        out_specs=pl.BlockSpec(memory_space=pltpu.VMEM),
        out_shape=jax.ShapeDtypeStruct(shape, BF16),
        compiler_params=vmem(48),
        name="out_grad",
    )(column, small, *attended, *cotangents)


def finish_output_body(mixed, weight, features, output, total):
    heads, size, rows = mixed.shape
    index = pl.program_id(0)

    @pl.when(index == 0)
    def _():
        total[...] = features[...].astype(F32)

    attended = mixed[...].reshape(heads * size, rows)
    total[...] += dot(attended, weight[...].reshape(heads * size, -1), 0, 0)

    @pl.when(index == pl.num_programs(0) - 1)
    def _():
        output[...] = total[...].astype(BF16)


def finish_output(mixed, weight, features):
    count, _, rows = mixed.shape
    _, size, width = weight.shape
    heads = 4
    return pl.pallas_call(
        finish_output_body,
        grid=(count // heads,),
        in_specs=[
            pl.BlockSpec((heads, size, rows), lambda i: (i, 0, 0)),
            pl.BlockSpec((heads, size, width), lambda i: (i, 0, 0)),
            whole((rows, width)),
        ],
        out_specs=whole((rows, width)),
        out_shape=jax.ShapeDtypeStruct((rows, width), BF16),
        scratch_shapes=[pltpu.VMEM((rows, width), F32)],
        compiler_params=vmem(60),
        cost_estimate=pl.CostEstimate(flops=1, bytes_accessed=1, transcendentals=0),
        name="finish_output",
    )(mixed, weight, features)


def finish_grad_body(mixed, weight, features, gain, cotangent, place, outgoing, total):
    heads, four, rows = mixed.shape
    size = four // 4
    index = pl.program_id(0)

    @pl.when(index == 0)
    def _():
        total[...] = jnp.zeros_like(total)

    grads = mixed[:, size:, :].reshape(heads * 3 * size, rows)
    total[...] += dot(grads, weight[...].reshape(heads * 3 * size, -1), 0, 0)

    @pl.when(index == pl.num_programs(0) - 1)
    def _():
        active = features[...].astype(F32)
        inverse = lax.rsqrt(jnp.mean(active * active, axis=1, keepdims=True) + EPSILON)
        scaled = gain[...] * total[...]
        cubed = inverse * inverse * inverse
        grad_active = inverse * scaled - active * cubed * jnp.mean(
            active * scaled, axis=1, keepdims=True
        )
        grad_features = (cotangent[...].astype(F32) + grad_active).astype(BF16)
        count = outgoing.shape[0] * outgoing.shape[1]
        slot = lax.broadcasted_iota(jnp.int32, (count, rows), 0)
        pick = jnp.where(slot == place[...], 1.0, 0.0).astype(BF16)
        outgoing[...] = dot(pick, grad_features, 1, 0).astype(BF16).reshape(outgoing.shape)


def finish_grad(mixed, weight, features, gain, cotangent, place, owners, slots):
    count, four, rows = mixed.shape
    width = features.shape[1]
    heads = 4
    return pl.pallas_call(
        finish_grad_body,
        grid=(count // heads,),
        in_specs=[
            pl.BlockSpec((heads, four, rows), lambda i: (i, 0, 0)),
            pl.BlockSpec((heads, four - four // 4, width), lambda i: (i, 0, 0)),
            whole((rows, width)),
            whole((1, width)),
            whole((rows, width)),
            whole((1, rows)),
        ],
        out_specs=whole((owners, slots, width)),
        out_shape=jax.ShapeDtypeStruct((owners, slots, width), BF16),
        scratch_shapes=[pltpu.VMEM((rows, width), F32)],
        compiler_params=vmem(60),
        name="finish_grad",
    )(mixed, weight, features, gain, cotangent, place)


def pick(value, k, axis=0):
    return lax.dynamic_index_in_dim(value, k, axis, keepdims=False)


def sum_to_tiles(value, small, tile_index):
    tiles, lines, lanes = value.shape
    ways = tiles // 2
    core, place = tile_index % 2, tile_index // 2
    value = value.reshape(ways, 2, lines, lanes)

    def mine(k):
        return pick(value, k, 1).reshape(ways * lines, lanes)

    other = jnp.concatenate([mine(1 - core), small], axis=0)
    other = lax.ppermute(other, "tile", [(i, i ^ 1) for i in range(tiles)])
    both = jnp.concatenate([mine(core), small], axis=0) + other
    value, small = both[: ways * lines].reshape(ways, lines, lanes), both[ways * lines :]
    parts = [jnp.concatenate([pick(value, place), small], axis=0)] + [
        lax.ppermute(
            jnp.concatenate([pick(value, (place + k) % ways), small], axis=0),
            "tile",
            [(i, (i + 2 * k) % tiles) for i in range(tiles)],
        )
        for k in range(1, ways)
    ]
    both = sum(parts[1:], parts[0])
    return both[:lines], both[lines:]


def on_device(
    tokens, levels, counts, level_table, norm_gain, project_weight, output_weight, cotangent
):
    tiles = lax.axis_size("tile")
    shards = lax.axis_size("seq")
    tile_index = lax.axis_index("tile")
    shard_index = lax.axis_index("seq")
    owners = tiles * shards
    slots = tokens.shape[3]
    width = tokens.shape[4]
    rows = cotangent.shape[1]
    length = rows * shards
    count, _, size, _ = project_weight.shape
    scale = 1.0 / math.sqrt(size)
    shift = math.log(length)
    factor = 1.0 / math.sqrt(tiles * length)
    kinds = level_table.shape[0]

    grad_rows = cotangent[0]
    side = math.isqrt(shards)
    line, column = shard_index // side, shard_index % side

    def along_line(value, k):
        return lax.ppermute(
            value, "seq", [(i, i // side * side + (i + k) % side) for i in range(shards)]
        )

    def along_column(value, k):
        return lax.ppermute(value, "seq", [(i, (i + k * side) % shards) for i in range(shards)])

    onehot = (levels[0][..., None] == jnp.arange(LANES, dtype=jnp.int32)).astype(BF16)
    embedded = tokens[0].astype(F32) + jnp.einsum(
        "msjl,ld->msjd", onehot[..., :kinds], level_table, preferred_element_type=F32
    )
    embedded = jnp.concatenate([embedded.astype(BF16), onehot], axis=-1)
    received = lax.all_to_all(
        embedded.reshape(owners, slots, width + LANES),
        ("tile", "seq"),
        split_axis=0,
        concat_axis=0,
        tiled=True,
    )
    map_counts = lax.dynamic_index_in_dim(counts, tile_index, 0, keepdims=False)
    own_counts = lax.dynamic_index_in_dim(map_counts, shard_index, 0, keepdims=False)
    place = pack_positions(own_counts, rows, slots)
    received, place_row = lax.optimization_barrier((received, place.reshape(1, rows)))
    gain = norm_gain.reshape(1, width)
    weight = project_weight.reshape(count, 3 * size, width)

    packed, features, normed, local = project(
        received,
        place.reshape(rows, 1),
        gain,
        grad_rows,
        weight,
        project_grads(grad_rows, output_weight),
    )
    by_head = lax.all_to_all(packed, "seq", split_axis=0, concat_axis=0, tiled=True)
    all_normed = lax.all_gather(normed, "seq")
    by_head, line_rows = lax.optimization_barrier((by_head, grad_rows))
    line_rows = [line_rows] + [along_line(line_rows, k) for k in range(1, side)]
    attended = attend(by_head, scale, shift)
    attended, line_rows = lax.optimization_barrier((attended, line_rows))
    mixed = lax.all_to_all(attended, "seq", split_axis=0, concat_axis=0, tiled=True)

    shares, small = weight_grad(
        shard_index.reshape(1),
        attended,
        by_head,
        all_normed,
        weight,
        gain,
        local,
        tiles,
        factor,
    )
    head_attended = attended.reshape(side, side, 4 * size, rows)[:, :, :size]
    column_attended = [pick(head_attended, line)] + [
        along_column(pick(head_attended, (line + k) % side), k) for k in range(1, side)
    ]
    out_shares = out_grad(column.reshape(1), small, column_attended, line_rows, factor)
    out_shares = sum(
        [along_column(out_shares[k], -k).astype(F32) for k in range(1, side)],
        out_shares[0].astype(F32),
    )
    outgoing = finish_grad(
        mixed, weight, features, gain, grad_rows, place_row, owners, slots
    )
    output = finish_output(mixed, output_weight, features)
    outgoing, out_shares, shares = lax.optimization_barrier((outgoing, out_shares, shares))
    returned = lax.all_to_all(
        outgoing,
        ("tile", "seq"),
        split_axis=0,
        concat_axis=0,
        tiled=True,
    )
    token_grad = returned.reshape(tiles, shards, slots, width)
    lines = tiles * size
    small_lines = (out_shares.shape[0] - lines) // 2
    small = out_shares[lines : lines + small_lines] + out_shares[lines + small_lines :]
    out_shares = out_shares[:lines].reshape(tiles, size, LANES)
    shares = jnp.concatenate([out_shares, shares.astype(F32)], axis=1)
    shares, small = sum_to_tiles(shares, small, tile_index)
    small = sum([along_line(small, k) for k in range(1, side)], small)
    small = small.reshape(width // LANES, LINES, LANES).transpose(1, 0, 2).reshape(LINES, width)
    return (
        output[None],
        token_grad[None],
        shares[size:].reshape(1, 3, size, width // tiles),
        shares[:size].reshape(1, size, width // tiles),
        small[LINES - 1],
        small[:kinds],
    )


def solution(mesh):
    return jax.shard_map(
        on_device,
        mesh=mesh,
        in_specs=(
            P(("tile", "seq"), None, None, None, None),
            P(("tile", "seq"), None, None, None),
            P(),
            P(),
            P(),
            P(),
            P(),
            P("tile", "seq", None),
        ),
        out_specs=(
            P("tile", "seq", None),
            P(("tile", "seq"), None, None, None, None),
            P("seq", None, None, "tile"),
            P("seq", None, "tile"),
            P(),
            P(),
        ),
        check_vma=False,
    )
```
